32 devices in a mesh: case: 2 (over y), region: 4 (over x, core), sub: 4 (over z).
Axes of the slice: x: 2, y: 2, z: 4, core: 2. Of those that a mesh axis runs over, the one named last changes fastest.
Arguments:
- vol_feat: bfloat16 [16384, 128], P(('case', 'region', 'sub')), parts along dimension 0, may hold values from -6 to 6
- cotangent: bfloat16 [16384, 512], P(('case', 'region', 'sub')), parts along dimension 0, may hold values from -6 to 6
- surface: bfloat16 [16384, 128], P(('case', 'sub')), parts along dimension 0, may hold values from -6 to 6
- enc_weight: bfloat16 [128, 512], replicated, may hold values from -0.5 to 0.5
- enc_bias: float32 [512], replicated, may hold values from -3 to 3
- in_weight: bfloat16 [128, 512], replicated, may hold values from -0.5 to 0.5
- mid_weight: bfloat16 [512, 512], replicated, may hold values from -0.25 to 0.25
- first_bias: float32 [512], replicated, may hold values from -3 to 3
- out_weight: bfloat16 [512, 512], replicated, may hold values from -0.25 to 0.25
- second_bias: float32 [512], replicated, may hold values from -3 to 3
- block_owner: int32 [32, 4], P(('case', 'region', 'sub')), parts along dimension 0, may hold values from 0 to 3, each once within a row
- block_local: int32 [32, 4], P(('case', 'region', 'sub')), parts along dimension 0, may hold values from 0 to 15
- block_count: int32 [32], P(('case', 'region', 'sub')), parts along dimension 0, may hold values from 1 to 4, as said below
- entry_row: int32 [32, 512], P(('case', 'region', 'sub')), parts along dimension 0, may hold values from 0 to 127
- entry_cell: int32 [32, 512], P(('case', 'region', 'sub')), parts along dimension 0, may hold values from 0 to 511
Outputs:
- grad_surface: float32 [16384, 128], P(('case', 'sub')), parts along dimension 0
- grad_enc_weight: bfloat16 [256, 512], P('case'), parts along dimension 0
- grad_enc_bias: float32 [1024], P('case'), parts along dimension 0
- grad_in_weight: bfloat16 [256, 512], P('case'), parts along dimension 0
- grad_mid_weight: bfloat16 [1024, 512], P('case'), parts along dimension 0
- grad_first_bias: float32 [1024], P('case'), parts along dimension 0
- grad_out_weight: bfloat16 [1024, 512], P('case'), parts along dimension 0
- grad_second_bias: float32 [1024], P('case'), parts along dimension 0
The draws below stay inside these ranges and needn't reach their ends.
There are 2 independent parts, one for each index of `case`. The reference program is written for one: setup_inputs(seed, part) draws one part's arguments, and reference() takes and returns one part's arrays. A program takes and returns all parts, laid end to end along the dimension named above; an argument that names none is the same for every part. Nothing has to cross between parts.
Inputs may be any that keep to these rules, and one draw needn't show every extreme that they name: `block_owner`: each row lists every sub index once. `block_count`: some device's count is 4.
All inputs are finite; a program needn't handle non-finite values.
Results may differ from the reference program's by a relative error of at most 0.0077.
Values may be sent and summed in bfloat16 or wider, within the bound.
No kernel may reach another device: no remote copies, remote signals or barrier semaphores. Data moves between devices by JAX's collectives and lax.ppermute only.
A program may use at most 64 MiB of HBM per device.

```python
import jax
import jax.numpy as jnp
from jax import lax

SC = 128
CIN = 128
H = 512
ROWS = 128
V_DEV = 512
SB_DEV = 16
VDEVS = 16
VCELLS = 8192
SROWS = 8192
N_REGION = 4
N_SUB = 4


def draw_block_count(key, part):
    key = jax.random.fold_in(key, 11)
    base_key, top_key = jax.random.split(key)
    counts = jax.random.randint(base_key, (N_REGION * N_SUB,), max(1, N_SUB // 8), N_SUB // 2 + 1)
    busiest = jax.random.randint(top_key, (), 0, N_REGION * N_SUB)
    return counts.at[busiest].set(N_SUB).astype(jnp.int32)


def touch_ends(entries, key, low, top_value):
    longest = entries.shape.index(max(entries.shape))
    spots = []
    for shift in (0, 1):
        where = [jax.random.randint(jax.random.fold_in(key, axis), (), 0, length) for axis, length in enumerate(entries.shape)]
        where[longest] = (where[longest] + shift) % entries.shape[longest]
        spots.append(tuple(where))
    return entries.at[spots[0]].set(low).at[spots[1]].set(top_value)


def steps_of(own_key, shape, cuts, low, high):
    loudness = 1.0
    for position, parts in cuts:
        heights = jax.random.uniform(jax.random.fold_in(jax.random.fold_in(own_key, 6), position), (parts,), jnp.float32, low / len(cuts), high / len(cuts))
        loudness = loudness * jnp.repeat(jnp.exp(heights), shape[position] // parts).reshape((-1,) + (1,) * (len(shape) - 1 - position))
    return loudness


def gaussian(stream_key, dims, scale, reach, pieces=(), kind=jnp.bfloat16):
    gain = steps_of(stream_key, dims, pieces, -0.22, 0.18) if pieces else 1.0
    values = jax.random.normal(stream_key, dims, jnp.float32) * scale * gain
    return jnp.minimum(jnp.maximum(values, -reach), reach).astype(kind)


def setup_inputs(seed: int = 0, part: int = 0) -> dict:
    splits = jax.random.split(jax.random.key(seed), 16)
    own_keys = jax.random.split(jax.random.fold_in(splits[15], part), 16)
    return {
        "vol_feat": gaussian(own_keys[0], (VCELLS, CIN), 1.0, 6.0, ((0, 16),)),
        "cotangent": gaussian(own_keys[1], (VCELLS, H), 1.0, 6.0, ((0, 16),)),
        "surface": gaussian(own_keys[2], (SROWS, SC), 1.0, 6.0, ((0, 4),)),
        "enc_weight": gaussian(splits[3], (SC, H), SC ** -0.5, 0.5),
        "enc_bias": gaussian(splits[4], (H,), 0.5, 3.0, (), jnp.float32),
        "in_weight": gaussian(splits[5], (CIN, H), CIN ** -0.5, 0.5),
        "mid_weight": gaussian(splits[6], (H, H), H ** -0.5, 0.25),
        "first_bias": gaussian(splits[7], (H,), 0.5, 3.0, (), jnp.float32),
        "out_weight": gaussian(splits[8], (H, H), H ** -0.5, 0.25),
        "second_bias": gaussian(splits[9], (H,), 0.5, 3.0, (), jnp.float32),
        "block_owner": jax.vmap(lambda own: jax.random.permutation(own, N_SUB))(jax.random.split(own_keys[10], VDEVS)).reshape((VDEVS, N_SUB)).astype(jnp.int32),
        "block_local": touch_ends(jax.random.randint(own_keys[11], (VDEVS, N_SUB), 0, SB_DEV), jax.random.fold_in(own_keys[11], 1), 0, SB_DEV - 1).astype(jnp.int32),
        "block_count": draw_block_count(jax.random.fold_in(jax.random.fold_in(splits[15], part), 71), part),
        "entry_row": touch_ends(jax.random.randint(own_keys[13], (VDEVS, N_SUB * ROWS), 0, ROWS), jax.random.fold_in(own_keys[13], 1), 0, ROWS - 1).astype(jnp.int32),
        "entry_cell": touch_ends(jax.random.randint(own_keys[14], (VDEVS, N_SUB * ROWS), 0, V_DEV), jax.random.fold_in(own_keys[14], 1), 0, V_DEV - 1).astype(jnp.int32),
    }


def gelu_slope(values):
    return jax.vjp(jax.nn.gelu, values)[1](jnp.ones_like(values))[0]

def reference(vol_feat, cotangent, surface, enc_weight, enc_bias, in_weight, mid_weight, first_bias, out_weight, second_bias, block_owner, block_local, block_count, entry_row, entry_cell):
    start_state = (jnp.zeros((SROWS, SC), jnp.float32), jnp.zeros((SC, H), jnp.float32), jnp.zeros((H,), jnp.float32), jnp.zeros((CIN, H), jnp.float32), jnp.zeros((H, H), jnp.float32), jnp.zeros((H,), jnp.float32), jnp.zeros((H, H), jnp.float32), jnp.zeros((H,), jnp.float32))

    def device_step(state, device_index):
        first_row = (device_index * V_DEV).astype(jnp.int32)
        inputs = lax.dynamic_slice_in_dim(vol_feat, first_row, V_DEV, 0)
        arriving = lax.dynamic_slice_in_dim(cotangent, first_row, V_DEV, 0)
        owners = block_owner[device_index]
        local_ids = block_local[device_index]
        live_blocks = (jnp.arange(N_SUB) < block_count[device_index]).astype(jnp.float32)
        entry_live = jnp.repeat(live_blocks, ROWS)
        global_block = owners * SB_DEV + local_ids
        rows_named = (jnp.repeat(global_block, ROWS) * ROWS + entry_row[device_index]).astype(jnp.int32)
        cells_named = entry_cell[device_index]
        gathered = jnp.take(surface, rows_named, axis=0)
        pre_act = jnp.dot(gathered, enc_weight, preferred_element_type=jnp.float32) + enc_bias
        neighbours = jax.ops.segment_sum(entry_live, cells_named, num_segments=V_DEV)
        cell_scale = 1.0 / jnp.maximum(neighbours, 1.0)
        activated = jax.nn.gelu(pre_act) * entry_live[:, None]
        encoded = (jax.ops.segment_sum(activated, cells_named, num_segments=V_DEV) * cell_scale[:, None]).astype(jnp.bfloat16)
        pre_first = jnp.dot(inputs, in_weight, preferred_element_type=jnp.float32) + jnp.dot(encoded, mid_weight, preferred_element_type=jnp.float32) + first_bias
        first_out = jax.nn.gelu(pre_first).astype(jnp.bfloat16)
        pre_second = jnp.dot(first_out, out_weight, preferred_element_type=jnp.float32) + second_bias
        grad_second = (arriving.astype(jnp.float32) * gelu_slope(pre_second)).astype(jnp.bfloat16)
        grad_first = (jnp.dot(grad_second, out_weight.T, preferred_element_type=jnp.float32) * gelu_slope(pre_first)).astype(jnp.bfloat16)
        cell_grad = jnp.dot(grad_first, mid_weight.T, preferred_element_type=jnp.float32) * cell_scale[:, None]
        entry_grad = (jnp.take(cell_grad, cells_named, axis=0) * gelu_slope(pre_act) * entry_live[:, None]).astype(jnp.bfloat16)
        row_grad = jnp.dot(entry_grad, enc_weight.T, preferred_element_type=jnp.float32)
        surf_acc, enc_w_acc, enc_b_acc, in_acc, mid_acc, first_acc, out_acc, second_acc = state
        surf_acc = surf_acc.at[rows_named].add(row_grad)
        enc_w_acc = enc_w_acc + jnp.dot(gathered.T, entry_grad, preferred_element_type=jnp.float32)
        enc_b_acc = enc_b_acc + lax.optimization_barrier(jnp.sum(entry_grad.astype(jnp.float32), axis=0))
        in_acc = in_acc + jnp.dot(inputs.T, grad_first, preferred_element_type=jnp.float32)
        mid_acc = mid_acc + jnp.dot(encoded.T, grad_first, preferred_element_type=jnp.float32)
        first_acc = first_acc + lax.optimization_barrier(jnp.sum(grad_first.astype(jnp.float32), axis=0))
        out_acc = out_acc + jnp.dot(first_out.T, grad_second, preferred_element_type=jnp.float32)
        second_acc = second_acc + lax.optimization_barrier(jnp.sum(grad_second.astype(jnp.float32), axis=0))
        return ((surf_acc, enc_w_acc, enc_b_acc, in_acc, mid_acc, first_acc, out_acc, second_acc), None)
    final_state, _ = lax.scan(device_step, start_state, jnp.arange(N_REGION * N_SUB, dtype=jnp.int32))
    surf_acc, enc_w_acc, enc_b_acc, in_acc, mid_acc, first_acc, out_acc, second_acc = final_state
    return (surf_acc, enc_w_acc.astype(jnp.bfloat16), enc_b_acc, in_acc.astype(jnp.bfloat16), mid_acc.astype(jnp.bfloat16), first_acc, out_acc.astype(jnp.bfloat16), second_acc)
```

```python
import functools

import jax
import jax.numpy as jnp
from jax import lax
from jax.experimental import pallas as pl
from jax.experimental.pallas import tpu as pltpu
from jax.sharding import PartitionSpec as P

BF16 = jnp.bfloat16
F32 = jnp.float32
VMEM = pl.BlockSpec(memory_space=pltpu.VMEM)
SMEM = pl.BlockSpec(memory_space=pltpu.SMEM)
ANY = pl.BlockSpec(memory_space=pl.ANY)
GROUP = 4
LIMIT = 48 * 1024 * 1024
PARAMS = pltpu.CompilerParams(vmem_limit_bytes=LIMIT)


def nn(a, b):
    return jnp.dot(a, b, preferred_element_type=F32)


def tn(a, b):
    return lax.dot_general(a, b, (((0,), (0,)), ((), ())), preferred_element_type=F32)


def nt(a, b):
    return lax.dot_general(a, b, (((1,), (1,)), ((), ())), preferred_element_type=F32)


def gelu_pair(v):
    square = v * v
    t = jnp.tanh(0.7978845608028654 * v * (1.0 + 0.044715 * square))
    half = 0.5 * (1.0 + t)
    inner = 0.7978845608028654 * (1.0 + 0.134145 * square)
    return v * half, half + 0.5 * v * (1.0 - t * t) * inner


def col_sum(a):
    return jnp.sum(a.astype(F32), axis=0, keepdims=True)


def loop(count, body):
    if count == 1:
        body(0)
    else:
        lax.fori_loop(0, count, lambda i, c: (body(i), c)[1], 0)


def serve_kernel(me_ref, *refs):
    count = (len(refs) - 3) // 2
    requests, surface, blocks = refs[:count], refs[count], refs[count + 1 : 2 * count + 1]
    ids_ref, sems = refs[2 * count + 1], refs[2 * count + 2]
    rows = blocks[0].shape[0]
    me = me_ref[0]
    copies = []
    for m, request in enumerate(requests):
        wanted = jnp.int32(0)
        for k in range(count):
            wanted = wanted + jnp.where(request[0, k] == me, request[0, count + k], 0)
        ids_ref[m] = wanted
        copy = pltpu.make_async_copy(
            surface.at[pl.ds(pl.multiple_of(wanted * rows, rows), rows), :], blocks[m], sems.at[m]
        )
        copy.start()
        copies.append(copy)
    for copy in copies:
        copy.wait()


def main_kernel(n_pieces, place_ref, owner_ref, count_ref, *refs):
    pieces = refs[:n_pieces]
    (
        row_ref,
        cell_ref,
        vol_ref,
        cot_ref,
        wenc_ref,
        benc_ref,
        win_ref,
        wmid_ref,
        b1_ref,
        wout_ref,
        b2_ref,
        keep_ref,
        send_ref,
        surf_ref,
        bias_ref,
        blocks,
        gathered_ref,
        slope_ref,
        hot_ref,
        total_ref,
        count_sum,
        wenc_sum,
        benc_sum,
    ) = refs[n_pieces:]
    half, mask = place_ref[0], place_ref[1]
    groups = row_ref.shape[0]
    cells, hidden = cot_ref.shape
    block_rows, channels = blocks.shape[1:]
    entries = GROUP * block_rows
    base = 0
    for piece in pieces:
        if len(piece.shape) == 2:
            blocks[base] = piece[...]
            base += 1
        else:
            blocks[...] = piece[...]
    live_count = count_ref[0]

    def row_hot(g, k):
        rows = lax.broadcasted_iota(jnp.int32, (block_rows, block_rows), 0)
        named = row_ref[g][:, k * block_rows : (k + 1) * block_rows]
        return (rows == named).astype(BF16)

    total_ref[...] = jnp.zeros_like(total_ref)
    count_sum[...] = jnp.zeros_like(count_sum)

    def encode(g):
        lane = lax.broadcasted_iota(jnp.int32, (1, entries), 1) // block_rows + g * GROUP
        named = jnp.where(lane < live_count, cell_ref[g], -1)
        hot = (lax.broadcasted_iota(jnp.int32, (cells, entries), 0) == named).astype(BF16)
        hot_ref[g] = hot
        for k in range(GROUP):
            block = blocks[owner_ref[g * GROUP + k] ^ mask]
            gathered_ref[g, k * block_rows : (k + 1) * block_rows, :] = tn(
                row_hot(g, k), block
            ).astype(BF16)
        act, slope = gelu_pair(nn(gathered_ref[g], wenc_ref[...]) + benc_ref[...])
        slope_ref[g] = slope
        total_ref[...] += nn(hot, act.astype(BF16))
        count_sum[...] += nn(hot, jnp.ones((entries, channels), BF16))

    loop(groups, encode)
    scale = 1.0 / jnp.maximum(count_sum[...], 1.0)
    scale = jnp.concatenate([scale] * (hidden // channels), axis=1)
    encoded = (total_ref[...] * scale).astype(BF16)
    pre_first = nn(vol_ref[...], win_ref[...]) + nn(encoded, wmid_ref[...]) + b1_ref[...]
    first, first_slope = gelu_pair(pre_first)
    first = first.astype(BF16)
    _, second_slope = gelu_pair(nn(first, wout_ref[...]) + b2_ref[...])
    grad_second = (cot_ref[...].astype(F32) * second_slope).astype(BF16)
    grad_first = (nt(grad_second, wout_ref[...]) * first_slope).astype(BF16)
    grad_cell = (nt(grad_first, wmid_ref[...]) * scale).astype(BF16)
    wenc_sum[...] = jnp.zeros_like(wenc_sum)
    benc_sum[...] = jnp.zeros_like(benc_sum)

    def reverse(g):
        grad_entry = (tn(hot_ref[g], grad_cell) * slope_ref[g]).astype(BF16)
        wenc_sum[...] += tn(gathered_ref[g], grad_entry)
        benc_sum[0:1, :] += col_sum(grad_entry)
        grad_row = nt(grad_entry, wenc_ref[...]).astype(BF16)
        for k in range(GROUP):
            grad_block = nn(row_hot(g, k), grad_row[k * block_rows : (k + 1) * block_rows, :])
            grad_block = grad_block.astype(BF16)
            slot = owner_ref[g * GROUP + k] ^ mask
            quarter = block_rows // 4
            for q in range(4):
                surf_ref[slot, :, q * channels : (q + 1) * channels] = grad_block[
                    q * quarter : (q + 1) * quarter, :
                ]

    loop(groups, reverse)
    benc_sum[1:2, :] = col_sum(grad_first)
    benc_sum[2:3, :] = col_sum(grad_second)
    sums = benc_sum[...]
    high = sums.astype(BF16).astype(F32)
    bias_ref[...] = jnp.concatenate([high, sums - high], axis=0).astype(BF16)

    def put(first_at, rows, values, twin=None):
        values = values.astype(BF16)
        low = values[: values.shape[0] // 2] if twin is None else values
        top = values[values.shape[0] // 2 :] if twin is None else twin.astype(BF16)

        @pl.when(half == 0)
        def _():
            for i in range(keep_ref.shape[0]):
                keep_ref[i, first_at : first_at + rows, :] = low[i * rows : (i + 1) * rows, :]
                send_ref[i, first_at : first_at + rows, :] = top[i * rows : (i + 1) * rows, :]

        @pl.when(half != 0)
        def _():
            for i in range(keep_ref.shape[0]):
                send_ref[i, first_at : first_at + rows, :] = low[i * rows : (i + 1) * rows, :]
                keep_ref[i, first_at : first_at + rows, :] = top[i * rows : (i + 1) * rows, :]

    put(0, 32, tn(first, grad_second))
    put(32, 32, tn(encoded, grad_first))
    put(64, 16, tn(vol_ref[...], grad_first), wenc_sum[...])


def halve_kernel(place_ref, keep_ref, got_ref, next_keep, next_send):
    mine = place_ref[0]
    quarter = next_keep.shape[0]
    for out, at in ((next_keep, mine), (next_send, 1 - mine)):
        rows = pl.ds(at * quarter, quarter)
        out[...] = (keep_ref[rows].astype(F32) + got_ref[rows].astype(F32)).astype(BF16)


def split_kernel(place_ref, keep_ref, got_ref, surf_ref, bias_ref, *outs):
    mine = place_ref[0]
    rows = keep_ref.shape[1]
    more = surf_ref.shape[1]
    for m, out in enumerate(outs):
        at = mine ^ m
        out[0:rows, :] = (keep_ref[at].astype(F32) + got_ref[at].astype(F32)).astype(BF16)
        out[rows : rows + more, :] = surf_ref[m]
        out[rows + more :, :] = bias_ref[...]


def sum_kernel(*refs):
    out = refs[-1]
    rows = out.shape[0]
    total = refs[0][0:rows, :].astype(F32)
    for ref in refs[1:-1]:
        total = total + ref[0:rows, :].astype(F32)
    out[...] = total.astype(BF16)


def join_kernel(*refs):
    out = refs[-1]
    count = out.shape[0]
    for m in range(count):
        rows = refs[m].shape[0]
        out[m, 0:rows, :] = refs[m][...]
        out[m, rows:, :] = refs[count + m][rows:, :]


def final_kernel(
    place_ref, ids_ref, own, over_x, over_core, over_both, surf, wenc, benc, win, wmid, b1, wout, b2
):
    c, x, z = place_ref[0], place_ref[1], place_ref[2]
    surf[...] = jnp.zeros_like(surf)
    block_rows, channels = surf.shape[1:]
    bias = None
    for at, (ref, core, chip) in enumerate(
        ((own, c, x), (over_x, c, 1 - x), (over_core, 1 - c, x), (over_both, 1 - c, 1 - x))
    ):
        for m in range(4):
            spot = chip * 4 + (z ^ m)
            shard = core * 8 + spot
            wout[pl.ds(pl.multiple_of(shard * 32, 32), 32), :] = ref[m, 0:32, :]
            wmid[pl.ds(pl.multiple_of(shard * 32, 32), 32), :] = ref[m, 32:64, :]
            narrow = pl.ds(pl.multiple_of(spot * 16, 16), 16)

            @pl.when(core == 0)
            def _():
                win[narrow, :] = ref[m, 64:80, :]

            @pl.when(core != 0)
            def _():
                wenc[narrow, :] = ref[m, 64:80, :]

            block = ids_ref[at, m]
            quarter = block_rows // 4
            for q in range(4):
                surf[block, q * quarter : (q + 1) * quarter, :] += ref[
                    m, 80:112, q * channels : (q + 1) * channels
                ].astype(F32)
            term = ref[m, 112:128, :].astype(F32)
            bias = term if bias is None else bias + term
    bias = bias[0:8, :] + bias[8:16, :]
    benc[...] = bias[0:1, :]
    b1[...] = bias[1:2, :]
    b2[...] = bias[2:3, :]


def call(kernel, out_shape, in_specs, *args, out_specs=None, scratch=(), flops=0):
    many = isinstance(out_shape, (list, tuple))
    return pl.pallas_call(
        kernel,
        out_shape=out_shape,
        in_specs=in_specs,
        out_specs=out_specs or ([VMEM] * len(out_shape) if many else VMEM),
        scratch_shapes=scratch,
        compiler_params=PARAMS,
        cost_estimate=pl.CostEstimate(flops=flops, bytes_accessed=1 << 20, transcendentals=0),
    )(*args)


def shape(dims, kind=BF16):
    return jax.ShapeDtypeStruct(dims, kind)


def compute(place, owner, count, pieces, entry_row, entry_cell, arrays):
    vol, cot, wenc, benc, win, wmid, b1, wout, b2 = arrays
    n_sub = owner.shape[0]
    block_rows = entry_row.shape[1] // n_sub
    cells, channels = vol.shape
    hidden = cot.shape[1]
    groups = n_sub // GROUP
    entries = GROUP * block_rows
    return call(
        functools.partial(main_kernel, len(pieces)),
        [
            shape((8, 80, hidden)),
            shape((8, 80, hidden)),
            shape((n_sub, block_rows // 4, hidden)),
            shape((16, hidden)),
        ],
        [SMEM] * 3 + [VMEM] * (len(pieces) + 11),
        place,
        owner,
        count,
        *pieces,
        entry_row.reshape(groups, 1, entries),
        entry_cell.reshape(groups, 1, entries),
        vol,
        cot,
        wenc,
        benc.reshape(1, hidden),
        win,
        wmid,
        b1.reshape(1, hidden),
        wout,
        b2.reshape(1, hidden),
        scratch=[
            pltpu.VMEM((n_sub, block_rows, channels), BF16),
            pltpu.VMEM((groups, entries, channels), BF16),
            pltpu.VMEM((groups, entries, hidden), F32),
            pltpu.VMEM((groups, cells, entries), BF16),
            pltpu.VMEM((cells, hidden), F32),
            pltpu.VMEM((cells, channels), F32),
            pltpu.VMEM((channels, hidden), F32),
            pltpu.VMEM((8, hidden), F32),
        ],
        flops=1 << 31,
    )


def swap(value, axis, mask, size):
    return lax.ppermute(value, axis, [(i, i ^ mask) for i in range(size)])


def on_block(surface, owner, local, count, entry_row, entry_cell, arrays):
    region, me = lax.axis_index("region"), lax.axis_index("sub")
    core, chip = region % 2, region // 2
    n_sub = owner.shape[0]
    block_rows = entry_row.shape[1] // n_sub
    channels = surface.shape[1]
    hidden = arrays[1].shape[1]
    along_z = range(1, n_sub)

    request = jnp.concatenate([owner, local]).reshape(1, 2 * n_sub)
    requests = [request] + [swap(request, "sub", m, n_sub) for m in along_z]
    *blocks, ids = call(
        serve_kernel,
        [shape((block_rows, channels))] * n_sub + [shape((n_sub,), jnp.int32)],
        [SMEM] * (n_sub + 1) + [ANY],
        me.reshape(1),
        *requests,
        surface,
        out_specs=[VMEM] * n_sub + [SMEM],
        scratch=[pltpu.SemaphoreType.DMA((n_sub,))],
    )
    blocks = [blocks[0]] + [swap(blocks[m], "sub", m, n_sub) for m in along_z]
    ids = ids.reshape(1, n_sub)
    ids = jnp.concatenate([ids, swap(ids, "region", 2, 4)])
    ids = jnp.concatenate([ids, swap(ids, "region", 1, 4)])

    keep, send, surf, bias = compute(
        jnp.stack([core, me]), owner, count, blocks, entry_row, entry_cell, arrays
    )
    got = swap(send, "region", 1, 4)
    keep, send = call(
        halve_kernel, [shape((4, 80, hidden))] * 2, [SMEM, VMEM, VMEM], chip.reshape(1), keep, got
    )
    got = swap(send, "region", 2, 4)
    messages = call(
        split_kernel,
        [shape((128, hidden))] * n_sub,
        [SMEM] + [VMEM] * 4,
        me.reshape(1),
        keep,
        got,
        surf,
        bias,
    )
    messages = [messages[0]] + [swap(messages[m], "sub", m, n_sub) for m in along_z]
    total = call(sum_kernel, shape((80, hidden)), [VMEM] * n_sub, *messages)
    totals = [total] + [swap(total, "sub", m, n_sub) for m in along_z]
    own = call(join_kernel, shape((n_sub, 128, hidden)), [VMEM] * (2 * n_sub), *totals, *messages)
    over_x = swap(own, "region", 2, 4)
    over_core = swap(own, "region", 1, 4)
    over_both = swap(over_x, "region", 1, 4)
    surf, wenc, benc, win, wmid, b1, wout, b2 = call(
        final_kernel,
        [
            shape((surface.shape[0] // block_rows, block_rows, channels), F32),
            shape((128, hidden)),
            shape((1, hidden), F32),
            shape((128, hidden)),
            shape((512, hidden)),
            shape((1, hidden), F32),
            shape((512, hidden)),
            shape((1, hidden), F32),
        ],
        [SMEM, SMEM] + [VMEM] * 4,
        jnp.stack([core, chip, me]),
        ids,
        own,
        over_x,
        over_core,
        over_both,
    )
    return (
        surf.reshape(surface.shape),
        wenc,
        benc.reshape(hidden),
        win,
        wmid,
        b1.reshape(hidden),
        wout,
        b2.reshape(hidden),
    )


def on_any(surface, owner, local, count, entry_row, entry_cell, arrays):
    n_sub = owner.shape[0]
    block_rows = entry_row.shape[1] // n_sub
    channels = surface.shape[1]
    hidden = arrays[1].shape[1]
    to_all = functools.partial(lax.all_to_all, axis_name="sub", split_axis=0, concat_axis=0, tiled=True)
    wanted = jnp.zeros((n_sub,), jnp.int32).at[owner].set(local)
    asked = to_all(wanted)
    stored = surface.reshape(surface.shape[0] // block_rows, block_rows, channels)
    fetched = to_all(jnp.take(stored, asked, axis=0))
    keep, send, surf, bias = compute(
        jnp.zeros((2,), jnp.int32), owner, count, [fetched], entry_row, entry_cell, arrays
    )
    surf = to_all(surf).astype(F32).reshape(n_sub, block_rows // 4, 4, channels)
    surf = surf.transpose(0, 2, 1, 3).reshape(n_sub, block_rows, channels)
    surf = jnp.zeros(stored.shape, F32).at[asked].add(surf).reshape(surface.shape)
    bias = bias[0:8].astype(F32) + bias[8:16].astype(F32)
    shards, bias = lax.psum(
        (jnp.concatenate([keep, send]).astype(F32), bias), ("region", "sub")
    )
    shards = shards.astype(BF16)
    small = shards[:, 64:80].reshape(256, hidden)
    return (
        lax.psum(surf, "region"),
        small[128:],
        bias[0],
        small[:128],
        shards[:, 32:64].reshape(512, hidden),
        bias[1],
        shards[:, 0:32].reshape(512, hidden),
        bias[2],
    )


def per_device(
    vol_feat,
    cotangent,
    surface,
    enc_weight,
    enc_bias,
    in_weight,
    mid_weight,
    first_bias,
    out_weight,
    second_bias,
    block_owner,
    block_local,
    block_count,
    entry_row,
    entry_cell,
):
    arrays = (
        vol_feat,
        cotangent,
        enc_weight,
        enc_bias,
        in_weight,
        mid_weight,
        first_bias,
        out_weight,
        second_bias,
    )
    small = lax.axis_size("region") == 4 and lax.axis_size("sub") == 4
    run = on_block if small else on_any
    return run(
        surface, block_owner[0], block_local[0], block_count, entry_row, entry_cell, arrays
    )


def solution(mesh):
    by_cell = P(("case", "region", "sub"), None)
    in_specs = (
        (by_cell, by_cell, P(("case", "sub"), None))
        + (P(),) * 7
        + (by_cell, by_cell, P(("case", "region", "sub")), by_cell, by_cell)
    )
    rows, line = P("case", None), P("case")
    out_specs = (P(("case", "sub"), None), rows, line, rows, rows, line, rows, line)
    return jax.shard_map(
        per_device, mesh=mesh, in_specs=in_specs, out_specs=out_specs, check_vma=False
    )
```

```python
import functools

import jax
import jax.numpy as jnp
from jax import lax
from jax.experimental import pallas as pl
from jax.experimental.pallas import tpu as pltpu
from jax.sharding import PartitionSpec as P

BF16 = jnp.bfloat16
F32 = jnp.float32
VMEM = pl.BlockSpec(memory_space=pltpu.VMEM)
SMEM = pl.BlockSpec(memory_space=pltpu.SMEM)
ANY = pl.BlockSpec(memory_space=pl.ANY)
HBM = pl.BlockSpec(memory_space=pltpu.HBM)
GROUP = 4
LIMIT = 16 * 1024 * 1024


def nn(a, b):
    return jnp.dot(a, b, preferred_element_type=F32)


def tn(a, b):
    return lax.dot_general(a, b, (((0,), (0,)), ((), ())), preferred_element_type=F32)


def nt(a, b):
    return lax.dot_general(a, b, (((1,), (1,)), ((), ())), preferred_element_type=F32)


def gelu_pair(v):
    square = v * v
    t = jnp.tanh(0.7978845608028654 * v * (1.0 + 0.044715 * square))
    half = 0.5 * (1.0 + t)
    inner = 0.7978845608028654 * (1.0 + 0.134145 * square)
    return v * half, half + 0.5 * v * (1.0 - t * t) * inner


def col_sum(a):
    return jnp.sum(a.astype(F32), axis=0, keepdims=True)


def loop(count, body):
    if count == 1:
        body(0)
    else:
        lax.fori_loop(0, count, lambda i, c: (body(i), c)[1], 0)


def serve_kernel(me_ref, *refs):
    count = (len(refs) - 4) // 2
    requests, surface, blocks = refs[:count], refs[count], refs[count + 2 : 2 * count + 2]
    ids_ref, sems = refs[2 * count + 2], refs[2 * count + 3]
    rows = blocks[0].shape[0]
    me = me_ref[0]
    copies = []
    for m, request in enumerate(requests):
        wanted = jnp.int32(0)
        for k in range(count):
            wanted = wanted + jnp.where(request[0, k] == me, request[0, count + k], 0)
        ids_ref[m] = wanted
        copy = pltpu.make_async_copy(
            surface.at[pl.ds(pl.multiple_of(wanted * rows, rows), rows), :], blocks[m], sems.at[m]
        )
        copy.start()
        copies.append(copy)
    for copy in copies:
        copy.wait()


def fill(out, surf_ref, bias, m):
    rows = surf_ref.shape[1]
    out[m, 0:rows, :] = surf_ref[m]
    out[m, rows:, :] = bias


def early_kernel(block_rows, count_ref, cell_ref, b1_ref, *refs):
    far, near = refs[:6], refs[6:11]
    hot_ref, scale_ref, base_ref, win_ref, sems = refs[11:]
    near = (win_ref,) + tuple(near)
    loads = [pltpu.make_async_copy(a, b, sems.at[i]) for i, (a, b) in enumerate(zip(far, near))]
    for load in loads:
        load.start()
    groups, cells, entries = hot_ref.shape
    channels = scale_ref.shape[1]
    live_count = count_ref[0]
    scale_ref[...] = jnp.zeros_like(scale_ref)

    def group(g):
        lane = lax.broadcasted_iota(jnp.int32, (1, entries), 1) // block_rows + g * GROUP
        named = jnp.where(lane < live_count, cell_ref[g], -1)
        hot = (lax.broadcasted_iota(jnp.int32, (cells, entries), 0) == named).astype(BF16)
        hot_ref[g] = hot
        scale_ref[...] += nn(hot, jnp.ones((entries, channels), BF16))

    loop(groups, group)
    scale_ref[...] = 1.0 / jnp.maximum(scale_ref[...], 1.0)
    loads[0].wait()
    loads[1].wait()
    base_ref[...] = nn(near[1][...], win_ref[...]) + b1_ref[...]
    for load in loads[2:]:
        load.wait()


def main_kernel(n_pieces, n_out, place_ref, owner_ref, *refs):
    pieces = refs[:n_pieces]
    row_ref, benc_ref, b2_ref = refs[n_pieces : n_pieces + 3]
    wenc_ref, vol_ref, wmid_ref, wout_ref, cot_ref = refs[n_pieces + 3 : n_pieces + 8]
    hot_ref, scale_ref, base_ref, keep_ref, send_ref = refs[n_pieces + 8 : n_pieces + 13]
    surf_refs = refs[n_pieces + 13 : n_pieces + 13 + n_out]
    blocks, gathered_ref, slope_ref, total_ref, wenc_sum, benc_sum, surf_ref = refs[
        n_pieces + 13 + n_out :
    ]
    half, mask = place_ref[0], place_ref[1]
    groups = row_ref.shape[0]
    cells, hidden = cot_ref.shape
    block_rows, channels = blocks.shape[1:]
    base = 0
    for piece in pieces:
        if len(piece.shape) == 2:
            blocks[base] = piece[...]
            base += 1
        else:
            blocks[...] = piece[...]

    def row_hot(g, k):
        rows = lax.broadcasted_iota(jnp.int32, (block_rows, block_rows), 0)
        named = row_ref[g][:, k * block_rows : (k + 1) * block_rows]
        return (rows == named).astype(BF16)

    total_ref[...] = jnp.zeros_like(total_ref)

    def encode(g):
        for k in range(GROUP):
            block = blocks[owner_ref[g * GROUP + k] ^ mask]
            gathered_ref[g, k * block_rows : (k + 1) * block_rows, :] = tn(
                row_hot(g, k), block
            ).astype(BF16)
        act, slope = gelu_pair(nn(gathered_ref[g], wenc_ref[...]) + benc_ref[...])
        slope_ref[g] = slope
        total_ref[...] += nn(hot_ref[g], act.astype(BF16))

    loop(groups, encode)
    scale = jnp.concatenate([scale_ref[...]] * (hidden // channels), axis=1)
    encoded = (total_ref[...] * scale).astype(BF16)
    pre_first = base_ref[...] + nn(encoded, wmid_ref[...])
    first, first_slope = gelu_pair(pre_first)
    first = first.astype(BF16)
    _, second_slope = gelu_pair(nn(first, wout_ref[...]) + b2_ref[...])
    grad_second = (cot_ref[...].astype(F32) * second_slope).astype(BF16)
    grad_first = (nt(grad_second, wout_ref[...]) * first_slope).astype(BF16)
    grad_cell = (nt(grad_first, wmid_ref[...]) * scale).astype(BF16)
    wenc_sum[...] = jnp.zeros_like(wenc_sum)
    benc_sum[...] = jnp.zeros_like(benc_sum)

    def reverse(g):
        grad_entry = (tn(hot_ref[g], grad_cell) * slope_ref[g]).astype(BF16)
        wenc_sum[...] += tn(gathered_ref[g], grad_entry)
        benc_sum[0:1, :] += col_sum(grad_entry)
        grad_row = nt(grad_entry, wenc_ref[...]).astype(BF16)
        for k in range(GROUP):
            grad_block = nn(row_hot(g, k), grad_row[k * block_rows : (k + 1) * block_rows, :])
            grad_block = grad_block.astype(BF16)
            slot = owner_ref[g * GROUP + k] ^ mask
            quarter = block_rows // 4
            for q in range(4):
                surf_ref[slot, :, q * channels : (q + 1) * channels] = grad_block[
                    q * quarter : (q + 1) * quarter, :
                ]

    loop(groups, reverse)
    benc_sum[1:2, :] = col_sum(grad_first)
    benc_sum[2:3, :] = col_sum(grad_second)
    sums = benc_sum[...]
    high = sums.astype(BF16).astype(F32)
    bias = jnp.concatenate([high, sums - high], axis=0).astype(BF16)
    rows = surf_ref.shape[1]
    for m, out in enumerate(surf_refs):
        if len(out.shape) == 2:
            out[0:rows, :] = surf_ref[m]
            out[rows:, :] = bias
        else:
            loop(out.shape[0], functools.partial(fill, out, surf_ref, bias))

    def put(first_at, rows, values, twin=None):
        values = values.astype(BF16)
        low = values[: values.shape[0] // 2] if twin is None else values
        top = values[values.shape[0] // 2 :] if twin is None else twin.astype(BF16)

        @pl.when(half == 0)
        def _():
            for i in range(keep_ref.shape[0]):
                keep_ref[i, first_at : first_at + rows, :] = low[i * rows : (i + 1) * rows, :]
                send_ref[i, first_at : first_at + rows, :] = top[i * rows : (i + 1) * rows, :]

        @pl.when(half != 0)
        def _():
            for i in range(keep_ref.shape[0]):
                send_ref[i, first_at : first_at + rows, :] = low[i * rows : (i + 1) * rows, :]
                keep_ref[i, first_at : first_at + rows, :] = top[i * rows : (i + 1) * rows, :]

    put(0, 32, tn(first, grad_second))
    put(32, 32, tn(encoded, grad_first))
    put(64, 16, tn(vol_ref[...], grad_first), wenc_sum[...])


def halve_kernel(place_ref, keep_ref, got_ref, next_keep, next_send):
    mine = place_ref[0]
    quarter = next_keep.shape[0]
    for out, at in ((next_keep, mine), (next_send, 1 - mine)):
        rows = pl.ds(at * quarter, quarter)
        out[...] = (keep_ref[rows].astype(F32) + got_ref[rows].astype(F32)).astype(BF16)


def split_kernel(place_ref, keep_ref, got_ref, _, *outs):
    mine = place_ref[0]
    for m, out in enumerate(outs):
        at = mine ^ m
        out[...] = (keep_ref[at].astype(F32) + got_ref[at].astype(F32)).astype(BF16)


def sum_kernel(_, *refs):
    total = refs[0][...].astype(F32)
    for ref in refs[1:-1]:
        total = total + ref[...].astype(F32)
    refs[-1][...] = total.astype(BF16)


def join_kernel(*refs):
    for m, ref in enumerate(refs[:-1]):
        refs[-1][m] = ref[...]


def label_kernel(ids_ref, *refs):
    out = refs[-1]
    for m, ref in enumerate(refs[:-1]):
        rows = ref.shape[0] - 16
        out[m, 0:rows, :] = ref[0:rows, :]
        place = lax.broadcasted_iota(jnp.int32, (16, ref.shape[1]), 0)
        tail = ref[rows:, :].astype(F32)
        out[m, rows:, :] = jnp.where(place == 3, ids_ref[m].astype(F32), tail).astype(BF16)


def surface_kernel(own, over_x, over_core, over_both, surf, benc, b1, b2):
    surf[...] = jnp.zeros_like(surf)
    block_rows, channels = surf.shape[1:]
    quarter = block_rows // 4
    bias = None
    for ref in (own, over_x, over_core, over_both):
        for m in range(ref.shape[0]):
            tail = ref[m, quarter:, :].astype(F32)
            block = jnp.max(tail[3:4, 0:channels]).astype(jnp.int32)
            for q in range(4):
                surf[block, q * quarter : (q + 1) * quarter, :] += ref[
                    m, 0:quarter, q * channels : (q + 1) * channels
                ].astype(F32)
            bias = tail if bias is None else bias + tail
    bias = bias[0:8, :] + bias[8:16, :]
    benc[...] = bias[0:1, :]
    b1[...] = bias[1:2, :]
    b2[...] = bias[2:3, :]


def weights_kernel(place_ref, own, over_x, over_core, over_both, wenc, win, wmid, wout):
    c, x, z = place_ref[0], place_ref[1], place_ref[2]
    for ref, core, chip in (
        (own, c, x),
        (over_x, c, 1 - x),
        (over_core, 1 - c, x),
        (over_both, 1 - c, 1 - x),
    ):
        for m in range(4):
            spot = chip * 4 + (z ^ m)
            shard = core * 8 + spot
            wout[pl.ds(pl.multiple_of(shard * 32, 32), 32), :] = ref[m, 0:32, :]
            wmid[pl.ds(pl.multiple_of(shard * 32, 32), 32), :] = ref[m, 32:64, :]
            narrow = pl.ds(pl.multiple_of(spot * 16, 16), 16)

            @pl.when(core == 0)
            def _():
                win[narrow, :] = ref[m, 64:80, :]

            @pl.when(core != 0)
            def _():
                wenc[narrow, :] = ref[m, 64:80, :]


def call(kernel, out_shape, in_specs, *args, out_specs=None, scratch=(), flops=0, limit=LIMIT):
    many = isinstance(out_shape, (list, tuple))
    return pl.pallas_call(
        kernel,
        out_shape=out_shape,
        in_specs=in_specs,
        out_specs=out_specs or ([VMEM] * len(out_shape) if many else VMEM),
        scratch_shapes=scratch,
        compiler_params=pltpu.CompilerParams(vmem_limit_bytes=limit),
        cost_estimate=pl.CostEstimate(flops=flops, bytes_accessed=1 << 20, transcendentals=0),
    )(*args)


def shape(dims, kind=BF16):
    return jax.ShapeDtypeStruct(dims, kind)


def prepare(count, entry_cell, n_sub, arrays):
    vol, cot, wenc, benc, win, wmid, b1, wout, b2 = arrays
    block_rows = entry_cell.shape[1] // n_sub
    cells, channels = vol.shape
    hidden = cot.shape[1]
    groups = n_sub // GROUP
    entries = GROUP * block_rows
    far = [pltpu.with_memory_space_constraint(a, pltpu.HBM) for a in (win, vol, wenc, wmid, wout, cot)]
    return call(
        functools.partial(early_kernel, block_rows),
        [shape(a.shape) for a in far[1:]]
        + [
            shape((groups, cells, entries)),
            shape((cells, channels), F32),
            shape((cells, hidden), F32),
        ],
        [SMEM, VMEM, VMEM] + [HBM] * 6,
        count,
        entry_cell.reshape(groups, 1, entries),
        b1.reshape(1, hidden),
        *far,
        scratch=[pltpu.VMEM(win.shape, BF16), pltpu.SemaphoreType.DMA((6,))],
        flops=1 << 30,
    )


def compute(place, owner, pieces, entry_row, early, arrays):
    vol, cot, wenc, benc, win, wmid, b1, wout, b2 = arrays
    n_sub = owner.shape[0]
    block_rows = entry_row.shape[1] // n_sub
    cells, channels = vol.shape
    hidden = cot.shape[1]
    groups = n_sub // GROUP
    entries = GROUP * block_rows
    message = (block_rows // 4 + 16, hidden)
    messages = [shape(message)] * n_sub if len(pieces) > 1 else [shape((n_sub,) + message)]
    near_vol, near_wenc, near_wmid, near_wout, near_cot, hot, scale, base = early
    keep, send, *messages = call(
        functools.partial(main_kernel, len(pieces), len(messages)),
        [shape((8, 80, hidden)), shape((8, 80, hidden))] + messages,
        [SMEM] * 2 + [VMEM] * (len(pieces) + 11),
        place,
        owner,
        *pieces,
        entry_row.reshape(groups, 1, entries),
        benc.reshape(1, hidden),
        b2.reshape(1, hidden),
        near_wenc,
        near_vol,
        near_wmid,
        near_wout,
        near_cot,
        hot,
        scale,
        base,
        scratch=[
            pltpu.VMEM((n_sub, block_rows, channels), BF16),
            pltpu.VMEM((groups, entries, channels), BF16),
            pltpu.VMEM((groups, entries, hidden), F32),
            pltpu.VMEM((cells, hidden), F32),
            pltpu.VMEM((channels, hidden), F32),
            pltpu.VMEM((8, hidden), F32),
            pltpu.VMEM((n_sub, block_rows // 4, hidden), BF16),
        ],
        flops=1 << 31,
        limit=32 * 1024 * 1024,
    )
    return keep, send, messages


def swap(value, axis, mask, size):
    return lax.ppermute(value, axis, [(i, i ^ mask) for i in range(size)])


def on_block(surface, owner, local, count, entry_row, entry_cell, arrays):
    region, me = lax.axis_index("region"), lax.axis_index("sub")
    core, chip = region % 2, region // 2
    n_sub = owner.shape[0]
    block_rows = entry_row.shape[1] // n_sub
    channels = surface.shape[1]
    hidden = arrays[1].shape[1]
    along_z = range(1, n_sub)

    request = jnp.concatenate([owner, local]).reshape(1, 2 * n_sub)
    requests = [request] + [swap(request, "sub", m, n_sub) for m in along_z]
    early = prepare(count, entry_cell, n_sub, arrays)
    *blocks, ids = call(
        serve_kernel,
        [shape((block_rows, channels))] * n_sub + [shape((n_sub,), jnp.int32)],
        [SMEM] * (n_sub + 1) + [HBM, ANY],
        me.reshape(1),
        *requests,
        pltpu.with_memory_space_constraint(surface, pltpu.HBM),
        early[6],
        out_specs=[VMEM] * n_sub + [SMEM],
        scratch=[pltpu.SemaphoreType.DMA((n_sub,))],
    )
    blocks = [blocks[0]] + [swap(blocks[m], "sub", m, n_sub) for m in along_z]
    keep, send, messages = compute(
        jnp.stack([core, me]), owner, blocks, entry_row, early, arrays
    )
    got = swap(send, "region", 1, 4)
    keep, send = call(
        halve_kernel, [shape((4, 80, hidden))] * 2, [SMEM, VMEM, VMEM], chip.reshape(1), keep, got
    )
    got = swap(send, "region", 2, 4)
    messages = [messages[0]] + [swap(messages[m], "sub", m, n_sub) for m in along_z]
    terms = call(
        label_kernel,
        shape((n_sub,) + messages[0].shape),
        [SMEM] + [VMEM] * n_sub,
        ids,
        *messages,
    )
    shards = call(
        split_kernel,
        [shape((80, hidden))] * n_sub,
        [SMEM, VMEM, VMEM, ANY],
        me.reshape(1),
        keep,
        got,
        terms,
    )
    shards = [shards[0]] + [swap(shards[m], "sub", m, n_sub) for m in along_z]
    terms_x = swap(terms, "region", 2, 4)
    terms_core = swap(terms, "region", 1, 4)
    terms_both = swap(terms_x, "region", 1, 4)
    surf, benc, b1, b2 = call(
        surface_kernel,
        [shape((surface.shape[0] // block_rows, block_rows, channels), F32)]
        + [shape((1, hidden), F32)] * 3,
        [VMEM] * 4,
        terms,
        terms_x,
        terms_core,
        terms_both,
    )
    total = call(sum_kernel, shape((80, hidden)), [ANY] + [VMEM] * n_sub, terms_x, *shards)
    totals = [total] + [swap(total, "sub", m, n_sub) for m in along_z]
    own = call(join_kernel, shape((n_sub, 80, hidden)), [VMEM] * n_sub, *totals)
    over_x = swap(own, "region", 2, 4)
    over_core = swap(own, "region", 1, 4)
    over_both = swap(over_x, "region", 1, 4)
    wenc, win, wmid, wout = call(
        weights_kernel,
        [shape((128, hidden)), shape((128, hidden)), shape((512, hidden)), shape((512, hidden))],
        [SMEM] + [VMEM] * 4,
        jnp.stack([core, chip, me]),
        own,
        over_x,
        over_core,
        over_both,
    )
    return (
        surf.reshape(surface.shape),
        wenc,
        benc.reshape(hidden),
        win,
        wmid,
        b1.reshape(hidden),
        wout,
        b2.reshape(hidden),
    )


def on_any(surface, owner, local, count, entry_row, entry_cell, arrays):
    n_sub = owner.shape[0]
    block_rows = entry_row.shape[1] // n_sub
    channels = surface.shape[1]
    hidden = arrays[1].shape[1]
    to_all = functools.partial(lax.all_to_all, axis_name="sub", split_axis=0, concat_axis=0, tiled=True)
    wanted = jnp.zeros((n_sub,), jnp.int32).at[owner].set(local)
    asked = to_all(wanted)
    stored = surface.reshape(surface.shape[0] // block_rows, block_rows, channels)
    fetched = to_all(jnp.take(stored, asked, axis=0))
    keep, send, (messages,) = compute(
        jnp.zeros((2,), jnp.int32),
        owner,
        [fetched],
        entry_row,
        prepare(count, entry_cell, n_sub, arrays),
        arrays,
    )
    bias = messages[0, block_rows // 4 :].astype(F32)
    bias = bias[0:8] + bias[8:16]
    surf = to_all(messages[:, : block_rows // 4]).astype(F32).reshape(n_sub, block_rows // 4, 4, channels)
    surf = surf.transpose(0, 2, 1, 3).reshape(n_sub, block_rows, channels)
    surf = jnp.zeros(stored.shape, F32).at[asked].add(surf).reshape(surface.shape)
    shards, bias = lax.psum(
        (jnp.concatenate([keep, send]).astype(F32), bias), ("region", "sub")
    )
    shards = shards.astype(BF16)
    small = shards[:, 64:80].reshape(256, hidden)
    return (
        lax.psum(surf, "region"),
        small[128:],
        bias[0],
        small[:128],
        shards[:, 32:64].reshape(512, hidden),
        bias[1],
        shards[:, 0:32].reshape(512, hidden),
        bias[2],
    )


def per_device(
    vol_feat,
    cotangent,
    surface,
    enc_weight,
    enc_bias,
    in_weight,
    mid_weight,
    first_bias,
    out_weight,
    second_bias,
    block_owner,
    block_local,
    block_count,
    entry_row,
    entry_cell,
):
    arrays = (
        vol_feat,
        cotangent,
        enc_weight,
        enc_bias,
        in_weight,
        mid_weight,
        first_bias,
        out_weight,
        second_bias,
    )
    small = lax.axis_size("region") == 4 and lax.axis_size("sub") == 4
    run = on_block if small else on_any
    return run(
        surface, block_owner[0], block_local[0], block_count, entry_row, entry_cell, arrays
    )


def solution(mesh):
    by_cell = P(("case", "region", "sub"), None)
    in_specs = (
        (by_cell, by_cell, P(("case", "sub"), None))
        + (P(),) * 7
        + (by_cell, by_cell, P(("case", "region", "sub")), by_cell, by_cell)
    )
    rows, line = P("case", None), P("case")
    out_specs = (P(("case", "sub"), None), rows, line, rows, rows, line, rows, line)
    return jax.shard_map(
        per_device, mesh=mesh, in_specs=in_specs, out_specs=out_specs, check_vma=False
    )
```

```python
import functools

import jax
import jax.numpy as jnp
from jax import lax
from jax.experimental import pallas as pl
from jax.experimental.pallas import tpu as pltpu
from jax.sharding import PartitionSpec as P

BF16 = jnp.bfloat16
F32 = jnp.float32
VMEM = pl.BlockSpec(memory_space=pltpu.VMEM)
SMEM = pl.BlockSpec(memory_space=pltpu.SMEM)
ANY = pl.BlockSpec(memory_space=pl.ANY)
HBM = pl.BlockSpec(memory_space=pltpu.HBM)
GROUP = 4
LIMIT = 16 * 1024 * 1024


def nn(a, b):
    return jnp.dot(a, b, preferred_element_type=F32)


def tn(a, b):
    return lax.dot_general(a, b, (((0,), (0,)), ((), ())), preferred_element_type=F32)


def nt(a, b):
    return lax.dot_general(a, b, (((1,), (1,)), ((), ())), preferred_element_type=F32)


def gelu_pair(v):
    square = v * v
    t = jnp.tanh(0.7978845608028654 * v * (1.0 + 0.044715 * square))
    half = 0.5 * (1.0 + t)
    inner = 0.7978845608028654 * (1.0 + 0.134145 * square)
    return v * half, half + 0.5 * v * (1.0 - t * t) * inner


def col_sum(a):
    return jnp.sum(a.astype(F32), axis=0, keepdims=True)


def loop(count, body):
    if count == 1:
        body(0)
    else:
        lax.fori_loop(0, count, lambda i, c: (body(i), c)[1], 0)


def serve_kernel(me_ref, *refs):
    count = (len(refs) - 3) // 2
    requests, surface, blocks = refs[:count], refs[count], refs[count + 1 : 2 * count + 1]
    ids_ref, sems = refs[2 * count + 1], refs[2 * count + 2]
    rows = blocks[0].shape[0]
    me = me_ref[0]
    copies = []
    for m, request in enumerate(requests):
        wanted = jnp.int32(0)
        for k in range(count):
            wanted = wanted + jnp.where(request[0, k] == me, request[0, count + k], 0)
        ids_ref[m] = wanted
        copy = pltpu.make_async_copy(
            surface.at[pl.ds(pl.multiple_of(wanted * rows, rows), rows), :], blocks[m], sems.at[m]
        )
        copy.start()
        copies.append(copy)
    for copy in copies:
        copy.wait()


def fill(out, surf_ref, bias, m):
    rows = surf_ref.shape[1]
    out[m, 0:rows, :] = surf_ref[m]
    out[m, rows:, :] = bias


def early_kernel(block_rows, count_ref, _, *refs):
    far, outs, sems = refs[:11], refs[11:22], refs[25]
    hot_ref, scale_ref, base_ref = outs[8:]
    cell_ref, win_ref, b1_ref = refs[22:25]
    near = (cell_ref, win_ref, b1_ref) + tuple(outs[:8])
    loads = [pltpu.make_async_copy(a, b, sems.at[i]) for i, (a, b) in enumerate(zip(far, near))]
    for load in loads:
        load.start()
    groups, cells, entries = hot_ref.shape
    channels = scale_ref.shape[1]
    live_count = count_ref[0]
    scale_ref[...] = jnp.zeros_like(scale_ref)
    loads[0].wait()

    def group(g):
        lane = lax.broadcasted_iota(jnp.int32, (1, entries), 1) // block_rows + g * GROUP
        named = jnp.where(lane < live_count, cell_ref[g], -1)
        hot = (lax.broadcasted_iota(jnp.int32, (cells, entries), 0) == named).astype(BF16)
        hot_ref[g] = hot
        scale_ref[...] += nn(hot, jnp.ones((entries, channels), BF16))

    loop(groups, group)
    scale_ref[...] = 1.0 / jnp.maximum(scale_ref[...], 1.0)
    for load in loads[1:4]:
        load.wait()
    base_ref[...] = nn(outs[0][...], win_ref[...]) + b1_ref[...]
    for load in loads[4:]:
        load.wait()


def row_hot(row_ref, block_rows, g, k):
    rows = lax.broadcasted_iota(jnp.int32, (block_rows, block_rows), 0)
    named = row_ref[g][:, k * block_rows : (k + 1) * block_rows]
    return (rows == named).astype(BF16)


def half_grads(which, out, early, made):
    vol_ref = early[0]
    first_ref, second_ref, encoded_ref, grad_first_ref, gathered_ref, entry_ref = made
    width = first_ref.shape[1] // 2
    columns = pl.ds(pl.multiple_of(which * width, width), width)
    for at, a, b in ((0, first_ref, second_ref), (32, encoded_ref, grad_first_ref)):
        values = tn(a[:, columns], b[...]).astype(BF16)
        for i in range(8):
            out[i, at : at + 32, :] = values[i * 32 : (i + 1) * 32, :]

    def narrow(values):
        values = values.astype(BF16)
        for i in range(8):
            out[i, 64:80, :] = values[i * 16 : (i + 1) * 16, :]

    @pl.when(which == 0)
    def _():
        narrow(tn(vol_ref[...], grad_first_ref[...]))

    @pl.when(which != 0)
    def _():
        groups = gathered_ref.shape[0]
        if groups == 1:
            narrow(tn(gathered_ref[0], entry_ref[0]))
        else:
            zero = jnp.zeros((gathered_ref.shape[2], entry_ref.shape[2]), F32)
            narrow(
                lax.fori_loop(
                    0, groups, lambda g, total: total + tn(gathered_ref[g], entry_ref[g]), zero
                )
            )


def main_kernel(n_pieces, n_out, place_ref, owner_ref, *refs):
    pieces, early = refs[:n_pieces], refs[n_pieces : n_pieces + 11]
    vol_ref, wenc_ref, wmid_ref, wout_ref, cot_ref, row_ref, benc_ref, b2_ref = early[:8]
    hot_ref, scale_ref, base_ref = early[8:]
    keep_ref, send_ref = refs[n_pieces + 11 : n_pieces + 13]
    outs = refs[n_pieces + 13 : n_pieces + 13 + n_out]
    made = refs[n_pieces + 13 + n_out : n_pieces + 19 + n_out]
    first_ref, second_ref, encoded_ref, grad_first_ref, gathered_ref, entry_ref = made
    blocks, slope_ref, total_ref, surf_ref, sums_ref = refs[n_pieces + 19 + n_out :]
    mask = place_ref[1]
    groups = row_ref.shape[0]
    hidden = cot_ref.shape[1]
    block_rows, channels = blocks.shape[1:]
    base = 0
    for piece in pieces:
        if len(piece.shape) == 2:
            blocks[base] = piece[...]
            base += 1
        else:
            blocks[...] = piece[...]
    total_ref[...] = jnp.zeros_like(total_ref)

    def encode(g):
        for k in range(GROUP):
            block = blocks[owner_ref[g * GROUP + k] ^ mask]
            gathered_ref[g, k * block_rows : (k + 1) * block_rows, :] = tn(
                row_hot(row_ref, block_rows, g, k), block
            ).astype(BF16)
        act, slope = gelu_pair(nn(gathered_ref[g], wenc_ref[...]) + benc_ref[...])
        slope_ref[g] = slope
        total_ref[...] += nn(hot_ref[g], act.astype(BF16))

    loop(groups, encode)
    scale = jnp.concatenate([scale_ref[...]] * (hidden // channels), axis=1)
    encoded = (total_ref[...] * scale).astype(BF16)
    encoded_ref[...] = encoded
    first, first_slope = gelu_pair(base_ref[...] + nn(encoded, wmid_ref[...]))
    first = first.astype(BF16)
    first_ref[...] = first
    _, second_slope = gelu_pair(nn(first, wout_ref[...]) + b2_ref[...])
    grad_second = (cot_ref[...].astype(F32) * second_slope).astype(BF16)
    second_ref[...] = grad_second
    grad_first = (nt(grad_second, wout_ref[...]) * first_slope).astype(BF16)
    grad_first_ref[...] = grad_first
    grad_cell = (nt(grad_first, wmid_ref[...]) * scale).astype(BF16)

    sums_ref[...] = jnp.zeros_like(sums_ref)

    def reverse(g):
        entry = (tn(hot_ref[g], grad_cell) * slope_ref[g]).astype(BF16)
        entry_ref[g] = entry
        sums_ref[0:1, :] += col_sum(entry)
        grad_row = nt(entry, wenc_ref[...]).astype(BF16)
        for k in range(GROUP):
            grad_block = nn(
                row_hot(row_ref, block_rows, g, k),
                grad_row[k * block_rows : (k + 1) * block_rows, :],
            ).astype(BF16)
            slot = owner_ref[g * GROUP + k] ^ mask
            quarter = block_rows // 4
            for q in range(4):
                surf_ref[slot, :, q * channels : (q + 1) * channels] = grad_block[
                    q * quarter : (q + 1) * quarter, :
                ]

    loop(groups, reverse)
    sums_ref[1:2, :] = col_sum(grad_first)
    sums_ref[2:3, :] = col_sum(grad_second)
    sums = sums_ref[...]
    high = sums.astype(BF16).astype(F32)
    bias = jnp.concatenate([high, sums - high], axis=0).astype(BF16)
    rows = surf_ref.shape[1]
    for m, out in enumerate(outs):
        if len(out.shape) == 2:
            out[0:rows, :] = surf_ref[m]
            out[rows:, :] = bias
        else:
            loop(out.shape[0], functools.partial(fill, out, surf_ref, bias))
    half_grads(1 - place_ref[0], send_ref, early, made)
    half_grads(place_ref[0], keep_ref, early, made)


def halve_kernel(place_ref, keep_ref, got_ref, next_keep, next_send):
    mine = place_ref[0]
    quarter = next_keep.shape[0]
    for out, at in ((next_keep, mine), (next_send, 1 - mine)):
        rows = pl.ds(at * quarter, quarter)
        out[...] = (keep_ref[rows].astype(F32) + got_ref[rows].astype(F32)).astype(BF16)


def split_kernel(place_ref, keep_ref, got_ref, *refs):
    mine, outs = place_ref[0], refs[3:]
    for m, out in enumerate(outs):
        at = mine ^ m
        out[...] = (keep_ref[at].astype(F32) + got_ref[at].astype(F32)).astype(BF16)


def sum_kernel(_, *refs):
    total = refs[0][...].astype(F32)
    for ref in refs[1:-1]:
        total = total + ref[...].astype(F32)
    refs[-1][...] = total.astype(BF16)


def join_kernel(*refs):
    for m, ref in enumerate(refs[:-1]):
        refs[-1][m] = ref[...]


def label_kernel(ids_ref, *refs):
    out = refs[-1]
    for m, ref in enumerate(refs[:-1]):
        rows = ref.shape[0] - 16
        out[m, 0:rows, :] = ref[0:rows, :]
        place = lax.broadcasted_iota(jnp.int32, (16, ref.shape[1]), 0)
        tail = ref[rows:, :].astype(F32)
        out[m, rows:, :] = jnp.where(place == 3, ids_ref[m].astype(F32), tail).astype(BF16)


def add_surface(groups, surf, benc, b1, b2):
    surf[...] = jnp.zeros_like(surf)
    block_rows, channels = surf.shape[1:]
    quarter = block_rows // 4
    sources = [ref.at[m] for ref in groups for m in range(ref.shape[0])]
    bias = None
    for ref in sources:
        tail = ref[quarter:, :].astype(F32)
        block = jnp.max(tail[3:4, 0:channels]).astype(jnp.int32)
        for q in range(4):
            surf[block, q * quarter : (q + 1) * quarter, :] += ref[
                0:quarter, q * channels : (q + 1) * channels
            ].astype(F32)
        bias = tail if bias is None else bias + tail
    bias = bias[0:8, :] + bias[8:16, :]
    benc[...] = bias[0:1, :]
    b1[...] = bias[1:2, :]
    b2[...] = bias[2:3, :]


def final_kernel(place_ref, own, over_x, over_core, over_both, *refs):
    surf, wenc, benc, win, wmid, b1, wout, b2 = refs[4:]
    add_surface(refs[:4], surf, benc, b1, b2)
    c, x, z = place_ref[0], place_ref[1], place_ref[2]
    pieces = []
    for m in range(4):
        pieces.append((own.at[m], c, x, m))
        pieces.append((over_x.at[m], c, 1 - x, m))
        pieces.append((over_core.at[m], 1 - c, x, m))
        pieces.append((over_both.at[m], 1 - c, 1 - x, m))
    for ref, at_core, at_chip, m in pieces:
        spot = at_chip * 4 + (z ^ m)
        wide = pl.ds(pl.multiple_of((at_core * 8 + spot) * 32, 32), 32)
        narrow = pl.ds(pl.multiple_of(spot * 16, 16), 16)
        wout[wide, :] = ref[0:32, :]
        wmid[wide, :] = ref[32:64, :]

        @pl.when(at_core == 0)
        def _():
            win[narrow, :] = ref[64:80, :]

        @pl.when(at_core != 0)
        def _():
            wenc[narrow, :] = ref[64:80, :]


def call(kernel, out_shape, in_specs, *args, out_specs=None, scratch=(), flops=0, limit=LIMIT):
    many = isinstance(out_shape, (list, tuple))
    return pl.pallas_call(
        kernel,
        out_shape=out_shape,
        in_specs=in_specs,
        out_specs=out_specs or ([VMEM] * len(out_shape) if many else VMEM),
        scratch_shapes=scratch,
        compiler_params=pltpu.CompilerParams(vmem_limit_bytes=limit),
        cost_estimate=pl.CostEstimate(flops=flops, bytes_accessed=1 << 20, transcendentals=0),
    )(*args)


def shape(dims, kind=BF16):
    return jax.ShapeDtypeStruct(dims, kind)


def prepare(count, after, entry_row, entry_cell, n_sub, arrays):
    vol, cot, wenc, benc, win, wmid, b1, wout, b2 = arrays
    block_rows = entry_cell.shape[1] // n_sub
    cells, channels = vol.shape
    hidden = cot.shape[1]
    groups = n_sub // GROUP
    entries = GROUP * block_rows
    rows, named = (a.reshape(groups, 1, entries) for a in (entry_row, entry_cell))
    benc, b1, b2 = (a.reshape(1, hidden) for a in (benc, b1, b2))
    far = (named, win, b1, vol, wenc, wmid, wout, cot, rows, benc, b2)
    far = [pltpu.with_memory_space_constraint(a, pltpu.HBM) for a in far]
    return call(
        functools.partial(early_kernel, block_rows),
        [shape(a.shape, a.dtype) for a in far[3:]]
        + [
            shape((groups, cells, entries)),
            shape((cells, channels), F32),
            shape((cells, hidden), F32),
        ],
        [SMEM, SMEM] + [HBM] * 11,
        count,
        after,
        *far,
        scratch=[pltpu.VMEM(a.shape, a.dtype) for a in far[:3]] + [pltpu.SemaphoreType.DMA((11,))],
        flops=1 << 30,
    )


def compute(place, owner, pieces, early, n_sub):
    vol, wenc, wmid, wout, cot, rows = early[:6]
    cells, channels = vol.shape
    hidden = cot.shape[1]
    groups, _, entries = rows.shape
    block_rows = entries // GROUP
    message = (block_rows // 4 + 16, hidden)
    messages = [shape(message)] * n_sub if len(pieces) > 1 else [shape((n_sub,) + message)]
    keep, send, *messages = call(
        functools.partial(main_kernel, len(pieces), len(messages)),
        [shape((8, 80, hidden))] * 2 + messages,
        [SMEM] * 2 + [VMEM] * (len(pieces) + 11),
        place,
        owner,
        *pieces,
        *early,
        scratch=[pltpu.VMEM((cells, hidden), BF16)] * 4
        + [
            pltpu.VMEM((groups, entries, channels), BF16),
            pltpu.VMEM((groups, entries, hidden), BF16),
            pltpu.VMEM((n_sub, block_rows, channels), BF16),
            pltpu.VMEM((groups, entries, hidden), F32),
            pltpu.VMEM((cells, hidden), F32),
            pltpu.VMEM((n_sub, block_rows // 4, hidden), BF16),
            pltpu.VMEM((8, hidden), F32),
        ],
        flops=1 << 31,
        limit=32 * 1024 * 1024,
    )
    return keep, send, messages


def swap(value, axis, mask, size):
    return lax.ppermute(value, axis, [(i, i ^ mask) for i in range(size)])


def on_block(surface, owner, local, count, entry_row, entry_cell, arrays):
    region, me = lax.axis_index("region"), lax.axis_index("sub")
    core, chip = region % 2, region // 2
    n_sub = owner.shape[0]
    block_rows = entry_row.shape[1] // n_sub
    channels = surface.shape[1]
    hidden = arrays[1].shape[1]
    along_z = range(1, n_sub)

    request = jnp.concatenate([owner, local]).reshape(1, 2 * n_sub)
    requests = [request] + [swap(request, "sub", m, n_sub) for m in along_z]
    *blocks, ids = call(
        serve_kernel,
        [shape((block_rows, channels))] * n_sub + [shape((n_sub,), jnp.int32)],
        [SMEM] * (n_sub + 1) + [HBM],
        me.reshape(1),
        *requests,
        pltpu.with_memory_space_constraint(surface, pltpu.HBM),
        out_specs=[VMEM] * n_sub + [SMEM],
        scratch=[pltpu.SemaphoreType.DMA((n_sub,))],
    )
    blocks = [blocks[0]] + [swap(blocks[m], "sub", m, n_sub) for m in along_z]
    early = prepare(count, ids, entry_row, entry_cell, n_sub, arrays)
    keep, send, messages = compute(jnp.stack([core, me]), owner, blocks, early, n_sub)
    got = swap(send, "region", 1, 4)
    keep, send = call(
        halve_kernel, [shape((4, 80, hidden))] * 2, [SMEM, VMEM, VMEM], chip.reshape(1), keep, got
    )
    got = swap(send, "region", 2, 4)
    messages = [messages[0]] + [swap(messages[m], "sub", m, n_sub) for m in along_z]
    terms = call(
        label_kernel,
        shape((n_sub,) + messages[0].shape),
        [SMEM] + [VMEM] * n_sub,
        ids,
        *messages,
    )
    shards = call(
        split_kernel,
        [shape((80, hidden))] * n_sub,
        [SMEM, VMEM, VMEM] + [ANY] * 3,
        me.reshape(1),
        keep,
        got,
        *messages[1:],
    )
    shards = [shards[0]] + [swap(shards[m], "sub", m, n_sub) for m in along_z]
    terms_x = swap(terms, "region", 2, 4)
    total = call(sum_kernel, shape((80, hidden)), [ANY] + [VMEM] * n_sub, terms_x, *shards)
    totals = [total] + [swap(total, "sub", m, n_sub) for m in along_z]
    terms = [terms, terms_x, swap(terms, "region", 1, 4), swap(terms_x, "region", 1, 4)]
    own = call(join_kernel, shape((n_sub, 80, hidden)), [VMEM] * n_sub, *totals)
    over_x = swap(own, "region", 2, 4)
    over_core = swap(own, "region", 1, 4)
    over_both = swap(over_x, "region", 1, 4)
    surf, wenc, benc, win, wmid, b1, wout, b2 = call(
        final_kernel,
        [
            shape((surface.shape[0] // block_rows, block_rows, channels), F32),
            shape((128, hidden)),
            shape((1, hidden), F32),
            shape((128, hidden)),
            shape((512, hidden)),
            shape((1, hidden), F32),
            shape((512, hidden)),
            shape((1, hidden), F32),
        ],
        [SMEM] + [VMEM] * 8,
        jnp.stack([core, chip, me]),
        own,
        over_x,
        over_core,
        over_both,
        *terms,
    )
    return (
        surf.reshape(surface.shape),
        wenc,
        benc.reshape(hidden),
        win,
        wmid,
        b1.reshape(hidden),
        wout,
        b2.reshape(hidden),
    )


def on_any(surface, owner, local, count, entry_row, entry_cell, arrays):
    n_sub = owner.shape[0]
    block_rows = entry_row.shape[1] // n_sub
    channels = surface.shape[1]
    hidden = arrays[1].shape[1]
    to_all = functools.partial(lax.all_to_all, axis_name="sub", split_axis=0, concat_axis=0, tiled=True)
    wanted = jnp.zeros((n_sub,), jnp.int32).at[owner].set(local)
    asked = to_all(wanted)
    stored = surface.reshape(surface.shape[0] // block_rows, block_rows, channels)
    fetched = to_all(jnp.take(stored, asked, axis=0))
    keep, send, (messages,) = compute(
        jnp.zeros((2,), jnp.int32),
        owner,
        [fetched],
        prepare(count, asked, entry_row, entry_cell, n_sub, arrays),
        n_sub,
    )
    bias = messages[0, block_rows // 4 :].astype(F32)
    bias = bias[0:8] + bias[8:16]
    surf = to_all(messages[:, : block_rows // 4]).astype(F32).reshape(n_sub, block_rows // 4, 4, channels)
    surf = surf.transpose(0, 2, 1, 3).reshape(n_sub, block_rows, channels)
    surf = jnp.zeros(stored.shape, F32).at[asked].add(surf).reshape(surface.shape)
    shards, bias = lax.psum(
        (jnp.concatenate([keep, send]).astype(F32), bias), ("region", "sub")
    )
    shards = shards.astype(BF16)
    small = shards[:, 64:80].reshape(256, hidden)
    return (
        lax.psum(surf, "region"),
        small[128:],
        bias[0],
        small[:128],
        shards[:, 32:64].reshape(512, hidden),
        bias[1],
        shards[:, 0:32].reshape(512, hidden),
        bias[2],
    )


def per_device(
    vol_feat,
    cotangent,
    surface,
    enc_weight,
    enc_bias,
    in_weight,
    mid_weight,
    first_bias,
    out_weight,
    second_bias,
    block_owner,
    block_local,
    block_count,
    entry_row,
    entry_cell,
):
    arrays = (
        vol_feat,
        cotangent,
        enc_weight,
        enc_bias,
        in_weight,
        mid_weight,
        first_bias,
        out_weight,
        second_bias,
    )
    small = lax.axis_size("region") == 4 and lax.axis_size("sub") == 4
    run = on_block if small else on_any
    return run(
        surface, block_owner[0], block_local[0], block_count, entry_row, entry_cell, arrays
    )


def solution(mesh):
    by_cell = P(("case", "region", "sub"), None)
    in_specs = (
        (by_cell, by_cell, P(("case", "sub"), None))
        + (P(),) * 7
        + (by_cell, by_cell, P(("case", "region", "sub")), by_cell, by_cell)
    )
    rows, line = P("case", None), P("case")
    out_specs = (P(("case", "sub"), None), rows, line, rows, rows, line, rows, line)
    return jax.shard_map(
        per_device, mesh=mesh, in_specs=in_specs, out_specs=out_specs, check_vma=False
    )
```

```python
import functools

import jax
import jax.numpy as jnp
from jax import lax
from jax.experimental import pallas as pl
from jax.experimental.pallas import tpu as pltpu
from jax.sharding import PartitionSpec as P

BF16 = jnp.bfloat16
F32 = jnp.float32
VMEM = pl.BlockSpec(memory_space=pltpu.VMEM)
SMEM = pl.BlockSpec(memory_space=pltpu.SMEM)
ANY = pl.BlockSpec(memory_space=pl.ANY)
HBM = pl.BlockSpec(memory_space=pltpu.HBM)
GROUP = 4
LIMIT = 16 * 1024 * 1024


def nn(a, b):
    return jnp.dot(a, b, preferred_element_type=F32)


def tn(a, b):
    return lax.dot_general(a, b, (((0,), (0,)), ((), ())), preferred_element_type=F32)


def nt(a, b):
    return lax.dot_general(a, b, (((1,), (1,)), ((), ())), preferred_element_type=F32)


def gelu_pair(v):
    square = v * v
    t = jnp.tanh(0.7978845608028654 * v * (1.0 + 0.044715 * square))
    half = 0.5 * (1.0 + t)
    inner = 0.7978845608028654 * (1.0 + 0.134145 * square)
    return v * half, half + 0.5 * v * (1.0 - t * t) * inner


def col_sum(a):
    return jnp.sum(a.astype(F32), axis=0, keepdims=True)


def loop(count, body):
    if count == 1:
        body(0)
    else:
        lax.fori_loop(0, count, lambda i, c: (body(i), c)[1], 0)


def serve_kernel(me_ref, *refs):
    count = (len(refs) - 2) // 2
    requests, surface, blocks = refs[:count], refs[count], refs[count + 1 : 2 * count + 1]
    ids_ref = refs[2 * count + 1]
    rows = blocks[0].shape[0]
    me = me_ref[0]
    for m, request in enumerate(requests):
        wanted = jnp.int32(0)
        for k in range(count):
            wanted = wanted + jnp.where(request[0, k] == me, request[0, count + k], 0)
        ids_ref[m] = wanted
        blocks[m][...] = surface[pl.ds(pl.multiple_of(wanted * rows, rows), rows), :]


def fill(out, surf_ref, bias, m):
    rows = surf_ref.shape[1]
    out[m, 0:rows, :] = surf_ref[m]
    out[m, rows:, :] = bias


def early_kernel(block_rows, count_ref, _, *refs):
    far, outs, sems = refs[:11], refs[11:22], refs[25]
    hot_ref, scale_ref, base_ref = outs[8:]
    cell_ref, win_ref, b1_ref = refs[22:25]
    near = (cell_ref, win_ref, b1_ref) + tuple(outs[:8])
    loads = [pltpu.make_async_copy(a, b, sems.at[i]) for i, (a, b) in enumerate(zip(far, near))]
    for load in loads:
        load.start()
    groups, cells, entries = hot_ref.shape
    channels = scale_ref.shape[1]
    live_count = count_ref[0]
    scale_ref[...] = jnp.zeros_like(scale_ref)
    loads[0].wait()

    def group(g):
        lane = lax.broadcasted_iota(jnp.int32, (1, entries), 1) // block_rows + g * GROUP
        named = jnp.where(lane < live_count, cell_ref[g], -1)
        hot = (lax.broadcasted_iota(jnp.int32, (cells, entries), 0) == named).astype(BF16)
        hot_ref[g] = hot
        scale_ref[...] += nn(hot, jnp.ones((entries, channels), BF16))

    loop(groups, group)
    scale_ref[...] = 1.0 / jnp.maximum(scale_ref[...], 1.0)
    for load in loads[1:4]:
        load.wait()
    base_ref[...] = nn(outs[0][...], win_ref[...]) + b1_ref[...]
    for load in loads[4:]:
        load.wait()


def row_hot(row_ref, block_rows, g, k):
    rows = lax.broadcasted_iota(jnp.int32, (block_rows, block_rows), 0)
    named = row_ref[g][:, k * block_rows : (k + 1) * block_rows]
    return (rows == named).astype(BF16)


def half_grads(which, out, early, made):
    vol_ref = early[0]
    first_ref, second_ref, encoded_ref, grad_first_ref, gathered_ref, entry_ref = made
    width = first_ref.shape[1] // 2
    columns = pl.ds(pl.multiple_of(which * width, width), width)
    for at, a, b in ((0, first_ref, second_ref), (32, encoded_ref, grad_first_ref)):
        values = tn(a[:, columns], b[...]).astype(BF16)
        for i in range(8):
            out[i, at : at + 32, :] = values[i * 32 : (i + 1) * 32, :]

    def narrow(values):
        values = values.astype(BF16)
        for i in range(8):
            out[i, 64:80, :] = values[i * 16 : (i + 1) * 16, :]

    @pl.when(which == 0)
    def _():
        narrow(tn(vol_ref[...], grad_first_ref[...]))

    @pl.when(which != 0)
    def _():
        groups = gathered_ref.shape[0]
        if groups == 1:
            narrow(tn(gathered_ref[0], entry_ref[0]))
        else:
            zero = jnp.zeros((gathered_ref.shape[2], entry_ref.shape[2]), F32)
            narrow(
                lax.fori_loop(
                    0, groups, lambda g, total: total + tn(gathered_ref[g], entry_ref[g]), zero
                )
            )


def main_kernel(n_pieces, n_out, place_ref, owner_ref, *refs):
    pieces, early = refs[:n_pieces], refs[n_pieces : n_pieces + 11]
    vol_ref, wenc_ref, wmid_ref, wout_ref, cot_ref, row_ref, benc_ref, b2_ref = early[:8]
    hot_ref, scale_ref, base_ref = early[8:]
    keep_ref, send_ref = refs[n_pieces + 11 : n_pieces + 13]
    outs = refs[n_pieces + 13 : n_pieces + 13 + n_out]
    made = refs[n_pieces + 13 + n_out : n_pieces + 19 + n_out]
    first_ref, second_ref, encoded_ref, grad_first_ref, gathered_ref, entry_ref = made
    blocks, slope_ref, total_ref, surf_ref, sums_ref = refs[n_pieces + 19 + n_out :]
    mask = place_ref[1]
    groups = row_ref.shape[0]
    hidden = cot_ref.shape[1]
    block_rows, channels = blocks.shape[1:]
    base = 0
    for piece in pieces:
        if len(piece.shape) == 2:
            blocks[base] = piece[...]
            base += 1
        else:
            blocks[...] = piece[...]
    total_ref[...] = jnp.zeros_like(total_ref)

    def encode(g):
        for k in range(GROUP):
            block = blocks[owner_ref[g * GROUP + k] ^ mask]
            gathered_ref[g, k * block_rows : (k + 1) * block_rows, :] = tn(
                row_hot(row_ref, block_rows, g, k), block
            ).astype(BF16)
        act, slope = gelu_pair(nn(gathered_ref[g], wenc_ref[...]) + benc_ref[...])
        slope_ref[g] = slope
        total_ref[...] += nn(hot_ref[g], act.astype(BF16))

    loop(groups, encode)
    scale = jnp.concatenate([scale_ref[...]] * (hidden // channels), axis=1)
    encoded = (total_ref[...] * scale).astype(BF16)
    encoded_ref[...] = encoded
    first, first_slope = gelu_pair(base_ref[...] + nn(encoded, wmid_ref[...]))
    first = first.astype(BF16)
    first_ref[...] = first
    _, second_slope = gelu_pair(nn(first, wout_ref[...]) + b2_ref[...])
    grad_second = (cot_ref[...].astype(F32) * second_slope).astype(BF16)
    second_ref[...] = grad_second
    grad_first = (nt(grad_second, wout_ref[...]) * first_slope).astype(BF16)
    grad_first_ref[...] = grad_first
    grad_cell = (nt(grad_first, wmid_ref[...]) * scale).astype(BF16)

    sums_ref[...] = jnp.zeros_like(sums_ref)

    def reverse(g):
        entry = (tn(hot_ref[g], grad_cell) * slope_ref[g]).astype(BF16)
        entry_ref[g] = entry
        sums_ref[0:1, :] += col_sum(entry)
        grad_row = nt(entry, wenc_ref[...]).astype(BF16)
        for k in range(GROUP):
            grad_block = nn(
                row_hot(row_ref, block_rows, g, k),
                grad_row[k * block_rows : (k + 1) * block_rows, :],
            ).astype(BF16)
            slot = owner_ref[g * GROUP + k] ^ mask
            quarter = block_rows // 4
            for q in range(4):
                surf_ref[slot, :, q * channels : (q + 1) * channels] = grad_block[
                    q * quarter : (q + 1) * quarter, :
                ]

    loop(groups, reverse)
    sums_ref[1:2, :] = col_sum(grad_first)
    sums_ref[2:3, :] = col_sum(grad_second)
    sums = sums_ref[...]
    high = sums.astype(BF16).astype(F32)
    bias = jnp.concatenate([high, sums - high], axis=0).astype(BF16)
    rows = surf_ref.shape[1]
    for m, out in enumerate(outs):
        if len(out.shape) == 2:
            out[0:rows, :] = surf_ref[m]
            out[rows:, :] = bias
        else:
            loop(out.shape[0], functools.partial(fill, out, surf_ref, bias))
    half_grads(1 - place_ref[0], send_ref, early, made)
    half_grads(place_ref[0], keep_ref, early, made)


def halve_kernel(place_ref, keep_ref, got_ref, next_keep, next_send):
    mine = place_ref[0]
    quarter = next_keep.shape[0]
    for out, at in ((next_keep, mine), (next_send, 1 - mine)):
        rows = pl.ds(at * quarter, quarter)
        out[...] = (keep_ref[rows].astype(F32) + got_ref[rows].astype(F32)).astype(BF16)


def split_kernel(place_ref, keep_ref, got_ref, *refs):
    mine, outs = place_ref[0], refs[3:]
    for m, out in enumerate(outs):
        at = mine ^ m
        out[...] = (keep_ref[at].astype(F32) + got_ref[at].astype(F32)).astype(BF16)


def sum_kernel(_, *refs):
    total = refs[0][...].astype(F32)
    for ref in refs[1:-1]:
        total = total + ref[...].astype(F32)
    refs[-1][...] = total.astype(BF16)


def join_kernel(*refs):
    for m, ref in enumerate(refs[:-1]):
        refs[-1][m] = ref[...]


def label_kernel(ids_ref, *refs):
    out = refs[-1]
    for m, ref in enumerate(refs[:-1]):
        rows = ref.shape[0] - 16
        out[m, 0:rows, :] = ref[0:rows, :]
        place = lax.broadcasted_iota(jnp.int32, (16, ref.shape[1]), 0)
        tail = ref[rows:, :].astype(F32)
        out[m, rows:, :] = jnp.where(place == 3, ids_ref[m].astype(F32), tail).astype(BF16)


def add_surface(groups, surf, benc, b1, b2):
    surf[...] = jnp.zeros_like(surf)
    block_rows, channels = surf.shape[1:]
    quarter = block_rows // 4
    sources = [ref.at[m] for ref in groups for m in range(ref.shape[0])]
    bias = None
    for ref in sources:
        tail = ref[quarter:, :].astype(F32)
        block = jnp.max(tail[3:4, 0:channels]).astype(jnp.int32)
        for q in range(4):
            surf[block, q * quarter : (q + 1) * quarter, :] += ref[
                0:quarter, q * channels : (q + 1) * channels
            ].astype(F32)
        bias = tail if bias is None else bias + tail
    bias = bias[0:8, :] + bias[8:16, :]
    benc[...] = bias[0:1, :]
    b1[...] = bias[1:2, :]
    b2[...] = bias[2:3, :]


def final_kernel(place_ref, own, over_x, over_core, over_both, *refs):
    surf, wenc, benc, win, wmid, b1, wout, b2 = refs[4:]
    add_surface(refs[:4], surf, benc, b1, b2)
    c, x, z = place_ref[0], place_ref[1], place_ref[2]
    pieces = []
    for m in range(4):
        pieces.append((own.at[m], c, x, m))
        pieces.append((over_x.at[m], c, 1 - x, m))
        pieces.append((over_core.at[m], 1 - c, x, m))
        pieces.append((over_both.at[m], 1 - c, 1 - x, m))
    for ref, at_core, at_chip, m in pieces:
        spot = at_chip * 4 + (z ^ m)
        wide = pl.ds(pl.multiple_of((at_core * 8 + spot) * 32, 32), 32)
        narrow = pl.ds(pl.multiple_of(spot * 16, 16), 16)
        wout[wide, :] = ref[0:32, :]
        wmid[wide, :] = ref[32:64, :]

        @pl.when(at_core == 0)
        def _():
            win[narrow, :] = ref[64:80, :]

        @pl.when(at_core != 0)
        def _():
            wenc[narrow, :] = ref[64:80, :]


def call(kernel, out_shape, in_specs, *args, out_specs=None, scratch=(), flops=0, limit=LIMIT):
    many = isinstance(out_shape, (list, tuple))
    return pl.pallas_call(
        kernel,
        out_shape=out_shape,
        in_specs=in_specs,
        out_specs=out_specs or ([VMEM] * len(out_shape) if many else VMEM),
        scratch_shapes=scratch,
        compiler_params=pltpu.CompilerParams(vmem_limit_bytes=limit),
        cost_estimate=pl.CostEstimate(flops=flops, bytes_accessed=1 << 20, transcendentals=0),
    )(*args)


def shape(dims, kind=BF16):
    return jax.ShapeDtypeStruct(dims, kind)


def prepare(count, after, entry_row, entry_cell, n_sub, arrays):
    vol, cot, wenc, benc, win, wmid, b1, wout, b2 = arrays
    block_rows = entry_cell.shape[1] // n_sub
    cells, channels = vol.shape
    hidden = cot.shape[1]
    groups = n_sub // GROUP
    entries = GROUP * block_rows
    rows, named = (a.reshape(groups, 1, entries) for a in (entry_row, entry_cell))
    benc, b1, b2 = (a.reshape(1, hidden) for a in (benc, b1, b2))
    far = (named, win, b1, vol, wenc, wmid, wout, cot, rows, benc, b2)
    far = [pltpu.with_memory_space_constraint(a, pltpu.HBM) for a in far]
    return call(
        functools.partial(early_kernel, block_rows),
        [shape(a.shape, a.dtype) for a in far[3:]]
        + [
            shape((groups, cells, entries)),
            shape((cells, channels), F32),
            shape((cells, hidden), F32),
        ],
        [SMEM, SMEM] + [HBM] * 11,
        count,
        after,
        *far,
        scratch=[pltpu.VMEM(a.shape, a.dtype) for a in far[:3]] + [pltpu.SemaphoreType.DMA((11,))],
        flops=1 << 30,
    )


def compute(place, owner, pieces, early, n_sub):
    vol, wenc, wmid, wout, cot, rows = early[:6]
    cells, channels = vol.shape
    hidden = cot.shape[1]
    groups, _, entries = rows.shape
    block_rows = entries // GROUP
    message = (block_rows // 4 + 16, hidden)
    messages = [shape(message)] * n_sub if len(pieces) > 1 else [shape((n_sub,) + message)]
    keep, send, *messages = call(
        functools.partial(main_kernel, len(pieces), len(messages)),
        [shape((8, 80, hidden))] * 2 + messages,
        [SMEM] * 2 + [VMEM] * (len(pieces) + 11),
        place,
        owner,
        *pieces,
        *early,
        scratch=[pltpu.VMEM((cells, hidden), BF16)] * 4
        + [
            pltpu.VMEM((groups, entries, channels), BF16),
            pltpu.VMEM((groups, entries, hidden), BF16),
            pltpu.VMEM((n_sub, block_rows, channels), BF16),
            pltpu.VMEM((groups, entries, hidden), F32),
            pltpu.VMEM((cells, hidden), F32),
            pltpu.VMEM((n_sub, block_rows // 4, hidden), BF16),
            pltpu.VMEM((8, hidden), F32),
        ],
        flops=1 << 31,
        limit=32 * 1024 * 1024,
    )
    return keep, send, messages


def swap(value, axis, mask, size):
    return lax.ppermute(value, axis, [(i, i ^ mask) for i in range(size)])


def on_block(surface, owner, local, count, entry_row, entry_cell, arrays):
    region, me = lax.axis_index("region"), lax.axis_index("sub")
    core, chip = region % 2, region // 2
    n_sub = owner.shape[0]
    block_rows = entry_row.shape[1] // n_sub
    channels = surface.shape[1]
    hidden = arrays[1].shape[1]
    along_z = range(1, n_sub)

    request = jnp.concatenate([owner, local]).reshape(1, 2 * n_sub)
    requests = [request] + [swap(request, "sub", m, n_sub) for m in along_z]
    near = swap(surface, "region", 1, 4)
    *blocks, ids = call(
        serve_kernel,
        [shape((block_rows, channels))] * n_sub + [shape((n_sub,), jnp.int32)],
        [SMEM] * (n_sub + 1) + [VMEM],
        me.reshape(1),
        *requests,
        near,
        out_specs=[VMEM] * n_sub + [SMEM],
    )
    blocks = [blocks[0]] + [swap(blocks[m], "sub", m, n_sub) for m in along_z]
    early = prepare(count, ids, entry_row, entry_cell, n_sub, arrays)
    keep, send, messages = compute(jnp.stack([core, me]), owner, blocks, early, n_sub)
    got = swap(send, "region", 1, 4)
    keep, send = call(
        halve_kernel, [shape((4, 80, hidden))] * 2, [SMEM, VMEM, VMEM], chip.reshape(1), keep, got
    )
    got = swap(send, "region", 2, 4)
    messages = [messages[0]] + [swap(messages[m], "sub", m, n_sub) for m in along_z]
    terms = call(
        label_kernel,
        shape((n_sub,) + messages[0].shape),
        [SMEM] + [VMEM] * n_sub,
        ids,
        *messages,
    )
    shards = call(
        split_kernel,
        [shape((80, hidden))] * n_sub,
        [SMEM, VMEM, VMEM] + [ANY] * 3,
        me.reshape(1),
        keep,
        got,
        *messages[1:],
    )
    shards = [shards[0]] + [swap(shards[m], "sub", m, n_sub) for m in along_z]
    terms_x = swap(terms, "region", 2, 4)
    total = call(sum_kernel, shape((80, hidden)), [ANY] + [VMEM] * n_sub, terms_x, *shards)
    totals = [total] + [swap(total, "sub", m, n_sub) for m in along_z]
    terms = [terms, terms_x, swap(terms, "region", 1, 4), swap(terms_x, "region", 1, 4)]
    own = call(join_kernel, shape((n_sub, 80, hidden)), [VMEM] * n_sub, *totals)
    over_x = swap(own, "region", 2, 4)
    over_core = swap(own, "region", 1, 4)
    over_both = swap(over_x, "region", 1, 4)
    surf, wenc, benc, win, wmid, b1, wout, b2 = call(
        final_kernel,
        [
            shape((surface.shape[0] // block_rows, block_rows, channels), F32),
            shape((128, hidden)),
            shape((1, hidden), F32),
            shape((128, hidden)),
            shape((512, hidden)),
            shape((1, hidden), F32),
            shape((512, hidden)),
            shape((1, hidden), F32),
        ],
        [SMEM] + [VMEM] * 8,
        jnp.stack([core, chip, me]),
        own,
        over_x,
        over_core,
        over_both,
        *terms,
    )
    return (
        surf.reshape(surface.shape),
        wenc,
        benc.reshape(hidden),
        win,
        wmid,
        b1.reshape(hidden),
        wout,
        b2.reshape(hidden),
    )


def on_any(surface, owner, local, count, entry_row, entry_cell, arrays):
    n_sub = owner.shape[0]
    block_rows = entry_row.shape[1] // n_sub
    channels = surface.shape[1]
    hidden = arrays[1].shape[1]
    to_all = functools.partial(lax.all_to_all, axis_name="sub", split_axis=0, concat_axis=0, tiled=True)
    wanted = jnp.zeros((n_sub,), jnp.int32).at[owner].set(local)
    asked = to_all(wanted)
    stored = surface.reshape(surface.shape[0] // block_rows, block_rows, channels)
    fetched = to_all(jnp.take(stored, asked, axis=0))
    keep, send, (messages,) = compute(
        jnp.zeros((2,), jnp.int32),
        owner,
        [fetched],
        prepare(count, asked, entry_row, entry_cell, n_sub, arrays),
        n_sub,
    )
    bias = messages[0, block_rows // 4 :].astype(F32)
    bias = bias[0:8] + bias[8:16]
    surf = to_all(messages[:, : block_rows // 4]).astype(F32).reshape(n_sub, block_rows // 4, 4, channels)
    surf = surf.transpose(0, 2, 1, 3).reshape(n_sub, block_rows, channels)
    surf = jnp.zeros(stored.shape, F32).at[asked].add(surf).reshape(surface.shape)
    shards, bias = lax.psum(
        (jnp.concatenate([keep, send]).astype(F32), bias), ("region", "sub")
    )
    shards = shards.astype(BF16)
    small = shards[:, 64:80].reshape(256, hidden)
    return (
        lax.psum(surf, "region"),
        small[128:],
        bias[0],
        small[:128],
        shards[:, 32:64].reshape(512, hidden),
        bias[1],
        shards[:, 0:32].reshape(512, hidden),
        bias[2],
    )


def per_device(
    vol_feat,
    cotangent,
    surface,
    enc_weight,
    enc_bias,
    in_weight,
    mid_weight,
    first_bias,
    out_weight,
    second_bias,
    block_owner,
    block_local,
    block_count,
    entry_row,
    entry_cell,
):
    arrays = (
        vol_feat,
        cotangent,
        enc_weight,
        enc_bias,
        in_weight,
        mid_weight,
        first_bias,
        out_weight,
        second_bias,
    )
    small = lax.axis_size("region") == 4 and lax.axis_size("sub") == 4
    run = on_block if small else on_any
    return run(
        surface, block_owner[0], block_local[0], block_count, entry_row, entry_cell, arrays
    )


def solution(mesh):
    by_cell = P(("case", "region", "sub"), None)
    in_specs = (
        (by_cell, by_cell, P(("case", "sub"), None))
        + (P(),) * 7
        + (by_cell, by_cell, P(("case", "region", "sub")), by_cell, by_cell)
    )
    rows, line = P("case", None), P("case")
    out_specs = (P(("case", "sub"), None), rows, line, rows, rows, line, rows, line)
    return jax.shard_map(
        per_device, mesh=mesh, in_specs=in_specs, out_specs=out_specs, check_vma=False
    )
```

```python
import functools

import jax
import jax.numpy as jnp
from jax import lax
from jax.experimental import pallas as pl
from jax.experimental.pallas import tpu as pltpu
from jax.sharding import PartitionSpec as P

BF16 = jnp.bfloat16
F32 = jnp.float32
VMEM = pl.BlockSpec(memory_space=pltpu.VMEM)
SMEM = pl.BlockSpec(memory_space=pltpu.SMEM)
ANY = pl.BlockSpec(memory_space=pl.ANY)
HBM = pl.BlockSpec(memory_space=pltpu.HBM)
GROUP = 4
LIMIT = 16 * 1024 * 1024


def nn(a, b):
    return jnp.dot(a, b, preferred_element_type=F32)


def tn(a, b):
    return lax.dot_general(a, b, (((0,), (0,)), ((), ())), preferred_element_type=F32)


def nt(a, b):
    return lax.dot_general(a, b, (((1,), (1,)), ((), ())), preferred_element_type=F32)


def gelu_pair(v):
    square = v * v
    t = jnp.tanh(0.7978845608028654 * v * (1.0 + 0.044715 * square))
    half = 0.5 * (1.0 + t)
    inner = 0.7978845608028654 * (1.0 + 0.134145 * square)
    return v * half, half + 0.5 * v * (1.0 - t * t) * inner


def col_sum(a):
    return jnp.sum(a.astype(F32), axis=0, keepdims=True)


def loop(count, body):
    if count == 1:
        body(0)
    else:
        lax.fori_loop(0, count, lambda i, c: (body(i), c)[1], 0)


def serve_kernel(me_ref, *refs):
    count = (len(refs) - 2) // 2
    requests, surface, blocks = refs[:count], refs[count], refs[count + 1 : 2 * count + 1]
    ids_ref = refs[2 * count + 1]
    rows = blocks[0].shape[0]
    me = me_ref[0]
    for m, request in enumerate(requests):
        wanted = jnp.int32(0)
        for k in range(count):
            wanted = wanted + jnp.where(request[0, k] == me, request[0, count + k], 0)
        ids_ref[m] = wanted
        blocks[m][...] = surface[pl.ds(pl.multiple_of(wanted * rows, rows), rows), :]


def fill(out, surf_ref, bias, m):
    rows = surf_ref.shape[1]
    out[m, 0:rows, :] = surf_ref[m]
    out[m, rows:, :] = bias


def early_kernel(block_rows, count_ref, _, *refs):
    far, outs, sems = refs[:11], refs[11:22], refs[25]
    hot_ref, scale_ref, base_ref = outs[8:]
    cell_ref, win_ref, b1_ref = refs[22:25]
    near = (cell_ref, win_ref, b1_ref) + tuple(outs[:8])
    loads = [pltpu.make_async_copy(a, b, sems.at[i]) for i, (a, b) in enumerate(zip(far, near))]
    for load in loads:
        load.start()
    groups, cells, entries = hot_ref.shape
    channels = scale_ref.shape[1]
    live_count = count_ref[0]
    scale_ref[...] = jnp.zeros_like(scale_ref)
    loads[0].wait()

    def group(g):
        lane = lax.broadcasted_iota(jnp.int32, (1, entries), 1) // block_rows + g * GROUP
        named = jnp.where(lane < live_count, cell_ref[g], -1)
        hot = (lax.broadcasted_iota(jnp.int32, (cells, entries), 0) == named).astype(BF16)
        hot_ref[g] = hot
        scale_ref[...] += nn(hot, jnp.ones((entries, channels), BF16))

    loop(groups, group)
    scale_ref[...] = 1.0 / jnp.maximum(scale_ref[...], 1.0)
    for load in loads[1:4]:
        load.wait()
    base_ref[...] = nn(outs[0][...], win_ref[...]) + b1_ref[...]
    for load in loads[4:]:
        load.wait()


def row_hot(row_ref, block_rows, g, k):
    rows = lax.broadcasted_iota(jnp.int32, (block_rows, block_rows), 0)
    named = row_ref[g][:, k * block_rows : (k + 1) * block_rows]
    return (rows == named).astype(BF16)


def half_grads(which, out, early, made):
    vol_ref = early[0]
    first_ref, second_ref, encoded_ref, grad_first_ref, gathered_ref, entry_ref = made
    width = first_ref.shape[1] // 2
    columns = pl.ds(pl.multiple_of(which * width, width), width)
    for at, a, b in ((0, first_ref, second_ref), (32, encoded_ref, grad_first_ref)):
        values = tn(a[:, columns], b[...]).astype(BF16)
        for i in range(8):
            out[i, at : at + 32, :] = values[i * 32 : (i + 1) * 32, :]

    def narrow(values):
        values = values.astype(BF16)
        for i in range(8):
            out[i, 64:80, :] = values[i * 16 : (i + 1) * 16, :]

    @pl.when(which == 0)
    def _():
        narrow(tn(vol_ref[...], grad_first_ref[...]))

    @pl.when(which != 0)
    def _():
        groups = gathered_ref.shape[0]
        if groups == 1:
            narrow(tn(gathered_ref[0], entry_ref[0]))
        else:
            zero = jnp.zeros((gathered_ref.shape[2], entry_ref.shape[2]), F32)
            narrow(
                lax.fori_loop(
                    0, groups, lambda g, total: total + tn(gathered_ref[g], entry_ref[g]), zero
                )
            )


def main_kernel(n_pieces, n_out, place_ref, owner_ref, *refs):
    pieces, early = refs[:n_pieces], refs[n_pieces : n_pieces + 11]
    vol_ref, wenc_ref, wmid_ref, wout_ref, cot_ref, row_ref, benc_ref, b2_ref = early[:8]
    hot_ref, scale_ref, base_ref = early[8:]
    keep_ref, send_ref = refs[n_pieces + 11 : n_pieces + 13]
    outs = refs[n_pieces + 13 : n_pieces + 13 + n_out]
    made = refs[n_pieces + 13 + n_out : n_pieces + 19 + n_out]
    first_ref, second_ref, encoded_ref, grad_first_ref, gathered_ref, entry_ref = made
    blocks, slope_ref, total_ref, surf_ref, sums_ref = refs[n_pieces + 19 + n_out :]
    mask = place_ref[1]
    groups = row_ref.shape[0]
    hidden = cot_ref.shape[1]
    block_rows, channels = blocks.shape[1:]
    base = 0
    for piece in pieces:
        if len(piece.shape) == 2:
            blocks[base] = piece[...]
            base += 1
        else:
            blocks[...] = piece[...]
    total_ref[...] = jnp.zeros_like(total_ref)

    def encode(g):
        for k in range(GROUP):
            block = blocks[owner_ref[g * GROUP + k] ^ mask]
            gathered_ref[g, k * block_rows : (k + 1) * block_rows, :] = tn(
                row_hot(row_ref, block_rows, g, k), block
            ).astype(BF16)
        act, slope = gelu_pair(nn(gathered_ref[g], wenc_ref[...]) + benc_ref[...])
        slope_ref[g] = slope
        total_ref[...] += nn(hot_ref[g], act.astype(BF16))

    loop(groups, encode)
    scale = jnp.concatenate([scale_ref[...]] * (hidden // channels), axis=1)
    encoded = (total_ref[...] * scale).astype(BF16)
    encoded_ref[...] = encoded
    first, first_slope = gelu_pair(base_ref[...] + nn(encoded, wmid_ref[...]))
    first = first.astype(BF16)
    first_ref[...] = first
    _, second_slope = gelu_pair(nn(first, wout_ref[...]) + b2_ref[...])
    grad_second = (cot_ref[...].astype(F32) * second_slope).astype(BF16)
    second_ref[...] = grad_second
    grad_first = (nt(grad_second, wout_ref[...]) * first_slope).astype(BF16)
    grad_first_ref[...] = grad_first
    grad_cell = (nt(grad_first, wmid_ref[...]) * scale).astype(BF16)

    sums_ref[...] = jnp.zeros_like(sums_ref)

    def reverse(g):
        entry = (tn(hot_ref[g], grad_cell) * slope_ref[g]).astype(BF16)
        entry_ref[g] = entry
        sums_ref[0:1, :] += col_sum(entry)
        grad_row = nt(entry, wenc_ref[...]).astype(BF16)
        for k in range(GROUP):
            grad_block = nn(
                row_hot(row_ref, block_rows, g, k),
                grad_row[k * block_rows : (k + 1) * block_rows, :],
            ).astype(BF16)
            slot = owner_ref[g * GROUP + k] ^ mask
            quarter = block_rows // 4
            for q in range(4):
                surf_ref[slot, :, q * channels : (q + 1) * channels] = grad_block[
                    q * quarter : (q + 1) * quarter, :
                ]

    loop(groups, reverse)
    sums_ref[1:2, :] = col_sum(grad_first)
    sums_ref[2:3, :] = col_sum(grad_second)
    sums = sums_ref[...]
    high = sums.astype(BF16).astype(F32)
    bias = jnp.concatenate([high, sums - high], axis=0).astype(BF16)
    rows = surf_ref.shape[1]
    for m, out in enumerate(outs):
        if len(out.shape) == 2:
            out[0:rows, :] = surf_ref[m]
            out[rows:, :] = bias
        else:
            loop(out.shape[0], functools.partial(fill, out, surf_ref, bias))
    half_grads(1 - place_ref[0], send_ref, early, made)
    half_grads(place_ref[0], keep_ref, early, made)


def halve_kernel(place_ref, keep_ref, got_ref, next_keep, next_send):
    mine = place_ref[0]
    quarter = next_keep.shape[0]
    for out, at in ((next_keep, mine), (next_send, 1 - mine)):
        rows = pl.ds(at * quarter, quarter)
        out[...] = (keep_ref[rows].astype(F32) + got_ref[rows].astype(F32)).astype(BF16)


def split_kernel(place_ref, keep_ref, got_ref, *refs):
    mine, outs = place_ref[0], refs[3:]
    for m, out in enumerate(outs):
        at = mine ^ m
        out[...] = (keep_ref[at].astype(F32) + got_ref[at].astype(F32)).astype(BF16)


def sum_kernel(_, *refs):
    total = refs[0][...].astype(F32)
    for ref in refs[1:-1]:
        total = total + ref[...].astype(F32)
    refs[-1][...] = total.astype(BF16)


def join_kernel(*refs):
    for m, ref in enumerate(refs[:-1]):
        refs[-1][m] = ref[...]


def label_kernel(ids_ref, *refs):
    out = refs[-1]
    for m, ref in enumerate(refs[:-1]):
        rows = ref.shape[0] - 16
        out[m, 0:rows, :] = ref[0:rows, :]
        place = lax.broadcasted_iota(jnp.int32, (16, ref.shape[1]), 0)
        tail = ref[rows:, :].astype(F32)
        out[m, rows:, :] = jnp.where(place == 3, ids_ref[m].astype(F32), tail).astype(BF16)


def surface_kernel(*refs):
    groups, own, surf, benc, b1, b2, passed = refs[:4], *refs[4:]
    passed[...] = own[...]
    surf[...] = jnp.zeros_like(surf)
    block_rows, channels = surf.shape[1:]
    quarter = block_rows // 4
    sources = [ref.at[m] for ref in groups for m in range(ref.shape[0])]
    bias = None
    for ref in sources:
        tail = ref[quarter:, :].astype(F32)
        block = jnp.max(tail[3:4, 0:channels]).astype(jnp.int32)
        for q in range(4):
            surf[block, q * quarter : (q + 1) * quarter, :] += ref[
                0:quarter, q * channels : (q + 1) * channels
            ].astype(F32)
        bias = tail if bias is None else bias + tail
    bias = bias[0:8, :] + bias[8:16, :]
    benc[...] = bias[0:1, :]
    b1[...] = bias[1:2, :]
    b2[...] = bias[2:3, :]


def weights_kernel(place_ref, own, over_x, over_core, over_both, wenc, win, wmid, wout):
    c, x, z = place_ref[0], place_ref[1], place_ref[2]
    pieces = []
    for m in range(4):
        pieces.append((own.at[m], c, x, m))
        pieces.append((over_x.at[m], c, 1 - x, m))
        pieces.append((over_core.at[m], 1 - c, x, m))
        pieces.append((over_both.at[m], 1 - c, 1 - x, m))
    for ref, at_core, at_chip, m in pieces:
        spot = at_chip * 4 + (z ^ m)
        wide = pl.ds(pl.multiple_of((at_core * 8 + spot) * 32, 32), 32)
        narrow = pl.ds(pl.multiple_of(spot * 16, 16), 16)
        wout[wide, :] = ref[0:32, :]
        wmid[wide, :] = ref[32:64, :]

        @pl.when(at_core == 0)
        def _():
            win[narrow, :] = ref[64:80, :]

        @pl.when(at_core != 0)
        def _():
            wenc[narrow, :] = ref[64:80, :]


def call(kernel, out_shape, in_specs, *args, out_specs=None, scratch=(), flops=0, limit=LIMIT):
    many = isinstance(out_shape, (list, tuple))
    return pl.pallas_call(
        kernel,
        out_shape=out_shape,
        in_specs=in_specs,
        out_specs=out_specs or ([VMEM] * len(out_shape) if many else VMEM),
        scratch_shapes=scratch,
        compiler_params=pltpu.CompilerParams(vmem_limit_bytes=limit),
        cost_estimate=pl.CostEstimate(flops=flops, bytes_accessed=1 << 20, transcendentals=0),
    )(*args)


def shape(dims, kind=BF16):
    return jax.ShapeDtypeStruct(dims, kind)


def prepare(count, after, entry_row, entry_cell, n_sub, arrays):
    vol, cot, wenc, benc, win, wmid, b1, wout, b2 = arrays
    block_rows = entry_cell.shape[1] // n_sub
    cells, channels = vol.shape
    hidden = cot.shape[1]
    groups = n_sub // GROUP
    entries = GROUP * block_rows
    rows, named = (a.reshape(groups, 1, entries) for a in (entry_row, entry_cell))
    benc, b1, b2 = (a.reshape(1, hidden) for a in (benc, b1, b2))
    far = (named, win, b1, vol, wenc, wmid, wout, cot, rows, benc, b2)
    far = [pltpu.with_memory_space_constraint(a, pltpu.HBM) for a in far]
    return call(
        functools.partial(early_kernel, block_rows),
        [shape(a.shape, a.dtype) for a in far[3:]]
        + [
            shape((groups, cells, entries)),
            shape((cells, channels), F32),
            shape((cells, hidden), F32),
        ],
        [SMEM, SMEM] + [HBM] * 11,
        count,
        after,
        *far,
        scratch=[pltpu.VMEM(a.shape, a.dtype) for a in far[:3]] + [pltpu.SemaphoreType.DMA((11,))],
        flops=1 << 30,
    )


def compute(place, owner, pieces, early, n_sub):
    vol, wenc, wmid, wout, cot, rows = early[:6]
    cells, channels = vol.shape
    hidden = cot.shape[1]
    groups, _, entries = rows.shape
    block_rows = entries // GROUP
    message = (block_rows // 4 + 16, hidden)
    messages = [shape(message)] * n_sub if len(pieces) > 1 else [shape((n_sub,) + message)]
    keep, send, *messages = call(
        functools.partial(main_kernel, len(pieces), len(messages)),
        [shape((8, 80, hidden))] * 2 + messages,
        [SMEM] * 2 + [VMEM] * (len(pieces) + 11),
        place,
        owner,
        *pieces,
        *early,
        scratch=[pltpu.VMEM((cells, hidden), BF16)] * 4
        + [
            pltpu.VMEM((groups, entries, channels), BF16),
            pltpu.VMEM((groups, entries, hidden), BF16),
            pltpu.VMEM((n_sub, block_rows, channels), BF16),
            pltpu.VMEM((groups, entries, hidden), F32),
            pltpu.VMEM((cells, hidden), F32),
            pltpu.VMEM((n_sub, block_rows // 4, hidden), BF16),
            pltpu.VMEM((8, hidden), F32),
        ],
        flops=1 << 31,
        limit=32 * 1024 * 1024,
    )
    return keep, send, messages


def swap(value, axis, mask, size):
    return lax.ppermute(value, axis, [(i, i ^ mask) for i in range(size)])


def on_block(surface, owner, local, count, entry_row, entry_cell, arrays):
    region, me = lax.axis_index("region"), lax.axis_index("sub")
    core, chip = region % 2, region // 2
    n_sub = owner.shape[0]
    block_rows = entry_row.shape[1] // n_sub
    channels = surface.shape[1]
    hidden = arrays[1].shape[1]
    along_z = range(1, n_sub)

    request = jnp.concatenate([owner, local]).reshape(1, 2 * n_sub)
    requests = [request] + [swap(request, "sub", m, n_sub) for m in along_z]
    near = swap(surface, "region", 1, 4)
    *blocks, ids = call(
        serve_kernel,
        [shape((block_rows, channels))] * n_sub + [shape((n_sub,), jnp.int32)],
        [SMEM] * (n_sub + 1) + [VMEM],
        me.reshape(1),
        *requests,
        near,
        out_specs=[VMEM] * n_sub + [SMEM],
    )
    blocks = [blocks[0]] + [swap(blocks[m], "sub", m, n_sub) for m in along_z]
    early = prepare(count, ids, entry_row, entry_cell, n_sub, arrays)
    keep, send, messages = compute(jnp.stack([core, me]), owner, blocks, early, n_sub)
    got = swap(send, "region", 1, 4)
    keep, send = call(
        halve_kernel, [shape((4, 80, hidden))] * 2, [SMEM, VMEM, VMEM], chip.reshape(1), keep, got
    )
    got = swap(send, "region", 2, 4)
    messages = [messages[0]] + [swap(messages[m], "sub", m, n_sub) for m in along_z]
    terms = call(
        label_kernel,
        shape((n_sub,) + messages[0].shape),
        [SMEM] + [VMEM] * n_sub,
        ids,
        *messages,
    )
    shards = call(
        split_kernel,
        [shape((80, hidden))] * n_sub,
        [SMEM, VMEM, VMEM] + [ANY] * 3,
        me.reshape(1),
        keep,
        got,
        *messages[1:],
    )
    shards = [shards[0]] + [swap(shards[m], "sub", m, n_sub) for m in along_z]
    terms_x = swap(terms, "region", 2, 4)
    total = call(sum_kernel, shape((80, hidden)), [ANY] + [VMEM] * n_sub, terms_x, *shards)
    totals = [total] + [swap(total, "sub", m, n_sub) for m in along_z]
    terms = [terms, terms_x, swap(terms, "region", 1, 4), swap(terms_x, "region", 1, 4)]
    own = call(join_kernel, shape((n_sub, 80, hidden)), [VMEM] * n_sub, *totals)
    over_x = swap(own, "region", 2, 4)
    surf, benc, b1, b2, passed = call(
        surface_kernel,
        [shape((surface.shape[0] // block_rows, block_rows, channels), F32)]
        + [shape((1, hidden), F32)] * 3
        + [shape(own.shape)],
        [VMEM] * 5,
        *terms,
        own,
    )
    over_core = swap(passed, "region", 1, 4)
    over_both = swap(over_x, "region", 1, 4)
    wenc, win, wmid, wout = call(
        weights_kernel,
        [shape((128, hidden)), shape((128, hidden)), shape((512, hidden)), shape((512, hidden))],
        [SMEM] + [VMEM] * 4,
        jnp.stack([core, chip, me]),
        own,
        over_x,
        over_core,
        over_both,
    )
    return (
        surf.reshape(surface.shape),
        wenc,
        benc.reshape(hidden),
        win,
        wmid,
        b1.reshape(hidden),
        wout,
        b2.reshape(hidden),
    )


def on_any(surface, owner, local, count, entry_row, entry_cell, arrays):
    n_sub = owner.shape[0]
    block_rows = entry_row.shape[1] // n_sub
    channels = surface.shape[1]
    hidden = arrays[1].shape[1]
    to_all = functools.partial(lax.all_to_all, axis_name="sub", split_axis=0, concat_axis=0, tiled=True)
    wanted = jnp.zeros((n_sub,), jnp.int32).at[owner].set(local)
    asked = to_all(wanted)
    stored = surface.reshape(surface.shape[0] // block_rows, block_rows, channels)
    fetched = to_all(jnp.take(stored, asked, axis=0))
    keep, send, (messages,) = compute(
        jnp.zeros((2,), jnp.int32),
        owner,
        [fetched],
        prepare(count, asked, entry_row, entry_cell, n_sub, arrays),
        n_sub,
    )
    bias = messages[0, block_rows // 4 :].astype(F32)
    bias = bias[0:8] + bias[8:16]
    surf = to_all(messages[:, : block_rows // 4]).astype(F32).reshape(n_sub, block_rows // 4, 4, channels)
    surf = surf.transpose(0, 2, 1, 3).reshape(n_sub, block_rows, channels)
    surf = jnp.zeros(stored.shape, F32).at[asked].add(surf).reshape(surface.shape)
    shards, bias = lax.psum(
        (jnp.concatenate([keep, send]).astype(F32), bias), ("region", "sub")
    )
    shards = shards.astype(BF16)
    small = shards[:, 64:80].reshape(256, hidden)
    return (
        lax.psum(surf, "region"),
        small[128:],
        bias[0],
        small[:128],
        shards[:, 32:64].reshape(512, hidden),
        bias[1],
        shards[:, 0:32].reshape(512, hidden),
        bias[2],
    )


def per_device(
    vol_feat,
    cotangent,
    surface,
    enc_weight,
    enc_bias,
    in_weight,
    mid_weight,
    first_bias,
    out_weight,
    second_bias,
    block_owner,
    block_local,
    block_count,
    entry_row,
    entry_cell,
):
    arrays = (
        vol_feat,
        cotangent,
        enc_weight,
        enc_bias,
        in_weight,
        mid_weight,
        first_bias,
        out_weight,
        second_bias,
    )
    small = lax.axis_size("region") == 4 and lax.axis_size("sub") == 4
    run = on_block if small else on_any
    return run(
        surface, block_owner[0], block_local[0], block_count, entry_row, entry_cell, arrays
    )


def solution(mesh):
    by_cell = P(("case", "region", "sub"), None)
    in_specs = (
        (by_cell, by_cell, P(("case", "sub"), None))
        + (P(),) * 7
        + (by_cell, by_cell, P(("case", "region", "sub")), by_cell, by_cell)
    )
    rows, line = P("case", None), P("case")
    out_specs = (P(("case", "sub"), None), rows, line, rows, rows, line, rows, line)
    return jax.shard_map(
        per_device, mesh=mesh, in_specs=in_specs, out_specs=out_specs, check_vma=False
    )
```

```python
import functools

import jax
import jax.numpy as jnp
from jax import lax
from jax.experimental import pallas as pl
from jax.experimental.pallas import tpu as pltpu
from jax.sharding import PartitionSpec as P

BF16 = jnp.bfloat16
F32 = jnp.float32
VMEM = pl.BlockSpec(memory_space=pltpu.VMEM)
SMEM = pl.BlockSpec(memory_space=pltpu.SMEM)
ANY = pl.BlockSpec(memory_space=pl.ANY)
HBM = pl.BlockSpec(memory_space=pltpu.HBM)
GROUP = 4
LIMIT = 16 * 1024 * 1024


def nn(a, b):
    return jnp.dot(a, b, preferred_element_type=F32)


def tn(a, b):
    return lax.dot_general(a, b, (((0,), (0,)), ((), ())), preferred_element_type=F32)


def nt(a, b):
    return lax.dot_general(a, b, (((1,), (1,)), ((), ())), preferred_element_type=F32)


def gelu_pair(v):
    square = v * v
    t = jnp.tanh(0.7978845608028654 * v * (1.0 + 0.044715 * square))
    half = 0.5 * (1.0 + t)
    inner = 0.7978845608028654 * (1.0 + 0.134145 * square)
    return v * half, half + 0.5 * v * (1.0 - t * t) * inner


def col_sum(a):
    return jnp.sum(a.astype(F32), axis=0, keepdims=True)


def loop(count, body):
    if count == 1:
        body(0)
    else:
        lax.fori_loop(0, count, lambda i, c: (body(i), c)[1], 0)


def serve_kernel(me_ref, *refs):
    count = (len(refs) - 2) // 2
    requests, surface, blocks = refs[:count], refs[count], refs[count + 1 : 2 * count + 1]
    ids_ref = refs[2 * count + 1]
    rows = blocks[0].shape[0]
    me = me_ref[0]
    for m, request in enumerate(requests):
        wanted = jnp.int32(0)
        for k in range(count):
            wanted = wanted + jnp.where(request[0, k] == me, request[0, count + k], 0)
        ids_ref[m] = wanted
        blocks[m][...] = surface[pl.ds(pl.multiple_of(wanted * rows, rows), rows), :]


def fill(out, surf_ref, bias, m):
    rows = surf_ref.shape[1]
    out[m, 0:rows, :] = surf_ref[m]
    out[m, rows:, :] = bias


def early_kernel(block_rows, count_ref, _, *refs):
    far, outs, sems = refs[:11], refs[11:22], refs[25]
    hot_ref, scale_ref, base_ref = outs[8:]
    cell_ref, win_ref, b1_ref = refs[22:25]
    near = (cell_ref, win_ref, b1_ref) + tuple(outs[:8])
    loads = [pltpu.make_async_copy(a, b, sems.at[i]) for i, (a, b) in enumerate(zip(far, near))]
    for load in loads:
        load.start()
    groups, cells, entries = hot_ref.shape
    channels = scale_ref.shape[1]
    live_count = count_ref[0]
    scale_ref[...] = jnp.zeros_like(scale_ref)
    loads[0].wait()

    def group(g):
        lane = lax.broadcasted_iota(jnp.int32, (1, entries), 1) // block_rows + g * GROUP
        named = jnp.where(lane < live_count, cell_ref[g], -1)
        hot = (lax.broadcasted_iota(jnp.int32, (cells, entries), 0) == named).astype(BF16)
        hot_ref[g] = hot
        scale_ref[...] += nn(hot, jnp.ones((entries, channels), BF16))

    loop(groups, group)
    scale_ref[...] = 1.0 / jnp.maximum(scale_ref[...], 1.0)
    for load in loads[1:4]:
        load.wait()
    base_ref[...] = nn(outs[0][...], win_ref[...]) + b1_ref[...]
    for load in loads[4:]:
        load.wait()


def row_hot(row_ref, block_rows, g, k):
    rows = lax.broadcasted_iota(jnp.int32, (block_rows, block_rows), 0)
    named = row_ref[g][:, k * block_rows : (k + 1) * block_rows]
    return (rows == named).astype(BF16)


def half_grads(which, out, early, made):
    vol_ref = early[0]
    first_ref, second_ref, encoded_ref, grad_first_ref, gathered_ref, entry_ref = made
    width = first_ref.shape[1] // 2
    columns = pl.ds(pl.multiple_of(which * width, width), width)
    for at, a, b in ((0, first_ref, second_ref), (32, encoded_ref, grad_first_ref)):
        values = tn(a[:, columns], b[...]).astype(BF16)
        for i in range(8):
            out[i, at : at + 32, :] = values[i * 32 : (i + 1) * 32, :]

    def narrow(values):
        values = values.astype(BF16)
        for i in range(8):
            out[i, 64:80, :] = values[i * 16 : (i + 1) * 16, :]

    @pl.when(which == 0)
    def _():
        narrow(tn(vol_ref[...], grad_first_ref[...]))

    @pl.when(which != 0)
    def _():
        groups = gathered_ref.shape[0]
        if groups == 1:
            narrow(tn(gathered_ref[0], entry_ref[0]))
        else:
            zero = jnp.zeros((gathered_ref.shape[2], entry_ref.shape[2]), F32)
            narrow(
                lax.fori_loop(
                    0, groups, lambda g, total: total + tn(gathered_ref[g], entry_ref[g]), zero
                )
            )


def main_kernel(n_pieces, n_out, place_ref, owner_ref, *refs):
    pieces, early = refs[:n_pieces], refs[n_pieces : n_pieces + 11]
    vol_ref, wenc_ref, wmid_ref, wout_ref, cot_ref, row_ref, benc_ref, b2_ref = early[:8]
    hot_ref, scale_ref, base_ref = early[8:]
    keep_ref, send_ref = refs[n_pieces + 11 : n_pieces + 13]
    outs = refs[n_pieces + 13 : n_pieces + 13 + n_out]
    made = refs[n_pieces + 13 + n_out : n_pieces + 19 + n_out]
    first_ref, second_ref, encoded_ref, grad_first_ref, gathered_ref, entry_ref = made
    blocks, slope_ref, total_ref, surf_ref, sums_ref = refs[n_pieces + 19 + n_out :]
    mask = place_ref[1]
    groups = row_ref.shape[0]
    hidden = cot_ref.shape[1]
    block_rows, channels = blocks.shape[1:]
    base = 0
    for piece in pieces:
        if len(piece.shape) == 2:
            blocks[base] = piece[...]
            base += 1
        else:
            blocks[...] = piece[...]
    total_ref[...] = jnp.zeros_like(total_ref)

    def encode(g):
        for k in range(GROUP):
            block = blocks[owner_ref[g * GROUP + k] ^ mask]
            gathered_ref[g, k * block_rows : (k + 1) * block_rows, :] = tn(
                row_hot(row_ref, block_rows, g, k), block
            ).astype(BF16)
        act, slope = gelu_pair(nn(gathered_ref[g], wenc_ref[...]) + benc_ref[...])
        slope_ref[g] = slope
        total_ref[...] += nn(hot_ref[g], act.astype(BF16))

    loop(groups, encode)
    scale = jnp.concatenate([scale_ref[...]] * (hidden // channels), axis=1)
    encoded = (total_ref[...] * scale).astype(BF16)
    encoded_ref[...] = encoded
    first, first_slope = gelu_pair(base_ref[...] + nn(encoded, wmid_ref[...]))
    first = first.astype(BF16)
    first_ref[...] = first
    _, second_slope = gelu_pair(nn(first, wout_ref[...]) + b2_ref[...])
    grad_second = (cot_ref[...].astype(F32) * second_slope).astype(BF16)
    second_ref[...] = grad_second
    grad_first = (nt(grad_second, wout_ref[...]) * first_slope).astype(BF16)
    grad_first_ref[...] = grad_first
    grad_cell = (nt(grad_first, wmid_ref[...]) * scale).astype(BF16)

    sums_ref[...] = jnp.zeros_like(sums_ref)

    def reverse(g):
        entry = (tn(hot_ref[g], grad_cell) * slope_ref[g]).astype(BF16)
        entry_ref[g] = entry
        sums_ref[0:1, :] += col_sum(entry)
        grad_row = nt(entry, wenc_ref[...]).astype(BF16)
        for k in range(GROUP):
            grad_block = nn(
                row_hot(row_ref, block_rows, g, k),
                grad_row[k * block_rows : (k + 1) * block_rows, :],
            ).astype(BF16)
            slot = owner_ref[g * GROUP + k] ^ mask
            quarter = block_rows // 4
            for q in range(4):
                surf_ref[slot, :, q * channels : (q + 1) * channels] = grad_block[
                    q * quarter : (q + 1) * quarter, :
                ]

    loop(groups, reverse)
    sums_ref[1:2, :] = col_sum(grad_first)
    sums_ref[2:3, :] = col_sum(grad_second)
    sums = sums_ref[...]
    high = sums.astype(BF16).astype(F32)
    bias = jnp.concatenate([high, sums - high], axis=0).astype(BF16)
    rows = surf_ref.shape[1]
    for m, out in enumerate(outs):
        if len(out.shape) == 2:
            out[0:rows, :] = surf_ref[m]
            out[rows:, :] = bias
        else:
            loop(out.shape[0], functools.partial(fill, out, surf_ref, bias))
    half_grads(1 - place_ref[0], send_ref, early, made)
    half_grads(place_ref[0], keep_ref, early, made)


def halve_kernel(place_ref, keep_ref, got_ref, next_keep, next_send):
    mine = place_ref[0]
    quarter = next_keep.shape[0]
    for out, at in ((next_keep, mine), (next_send, 1 - mine)):
        rows = pl.ds(at * quarter, quarter)
        out[...] = (keep_ref[rows].astype(F32) + got_ref[rows].astype(F32)).astype(BF16)


def split_kernel(place_ref, keep_ref, got_ref, *refs):
    mine, outs = place_ref[0], refs[3:]
    for m, out in enumerate(outs):
        at = mine ^ m
        out[...] = (keep_ref[at].astype(F32) + got_ref[at].astype(F32)).astype(BF16)


def sum_kernel(_, *refs):
    total = refs[0][...].astype(F32)
    for ref in refs[1:-1]:
        total = total + ref[...].astype(F32)
    refs[-1][...] = total.astype(BF16)


def join_kernel(place_ref, *refs):
    for m, ref in enumerate(refs[:-1]):
        refs[-1][place_ref[0] ^ m] = ref[...]


def label_kernel(ids_ref, *refs):
    out = refs[-1]
    for m, ref in enumerate(refs[:-1]):
        rows = ref.shape[0] - 16
        out[m, 0:rows, :] = ref[0:rows, :]
        place = lax.broadcasted_iota(jnp.int32, (16, ref.shape[1]), 0)
        tail = ref[rows:, :].astype(F32)
        out[m, rows:, :] = jnp.where(place == 3, ids_ref[m].astype(F32), tail).astype(BF16)


def surface_kernel(*refs):
    groups, own, surf, benc, b1, b2, passed = refs[:4], *refs[4:]
    passed[...] = own[...]
    surf[...] = jnp.zeros_like(surf)
    block_rows, channels = surf.shape[1:]
    quarter = block_rows // 4
    sources = [ref.at[m] for ref in groups for m in range(ref.shape[0])]
    bias = None
    for ref in sources:
        tail = ref[quarter:, :].astype(F32)
        block = jnp.max(tail[3:4, 0:channels]).astype(jnp.int32)
        for q in range(4):
            surf[block, q * quarter : (q + 1) * quarter, :] += ref[
                0:quarter, q * channels : (q + 1) * channels
            ].astype(F32)
        bias = tail if bias is None else bias + tail
    bias = bias[0:8, :] + bias[8:16, :]
    benc[...] = bias[0:1, :]
    b1[...] = bias[1:2, :]
    b2[...] = bias[2:3, :]


def place_shards(sources, outs, sems):
    wenc, win, wmid, wout = outs
    copies = []
    for i, (ref, at_core, at_chip) in enumerate(sources):
        count = ref.shape[0]
        wide = pl.ds((at_core * 2 + at_chip) * count, count)
        narrow = pl.ds(at_chip * count, count)
        for k, (rows, out, where, on) in enumerate(
            (
                (pl.ds(0, 32), wout, wide, None),
                (pl.ds(32, 32), wmid, wide, None),
                (pl.ds(64, 16), win, narrow, at_core == 0),
                (pl.ds(64, 16), wenc, narrow, at_core != 0),
            )
        ):
            copy = pltpu.make_async_copy(
                ref.at[:, rows, :], out.at[where], sems.at[i * 3 + min(k, 2)]
            )
            copies.append((copy, on))
    for copy, on in copies:
        if on is None:
            copy.start()
        else:
            pl.when(on)(copy.start)
    for copy, on in copies:
        if on is None:
            copy.wait()
        else:
            pl.when(on)(copy.wait)


def weights_kernel(place_ref, own, over_x, over_core, *refs):
    c, x = place_ref[0], place_ref[1]
    place_shards(((own, c, x), (over_x, c, 1 - x), (over_core, 1 - c, x)), refs[:4], refs[4])


def last_weights_kernel(place_ref, over_both, *refs):
    c, x = place_ref[0], place_ref[1]
    place_shards(((over_both, 1 - c, 1 - x),), refs[4:8], refs[8])


def call(kernel, out_shape, in_specs, *args, out_specs=None, scratch=(), flops=0, limit=LIMIT, aliases=None):
    many = isinstance(out_shape, (list, tuple))
    return pl.pallas_call(
        kernel,
        out_shape=out_shape,
        in_specs=in_specs,
        out_specs=out_specs or ([VMEM] * len(out_shape) if many else VMEM),
        scratch_shapes=scratch,
        input_output_aliases=aliases or {},
        compiler_params=pltpu.CompilerParams(vmem_limit_bytes=limit),
        cost_estimate=pl.CostEstimate(flops=flops, bytes_accessed=1 << 20, transcendentals=0),
    )(*args)


def shape(dims, kind=BF16):
    return jax.ShapeDtypeStruct(dims, kind)


def prepare(count, after, entry_row, entry_cell, n_sub, arrays):
    vol, cot, wenc, benc, win, wmid, b1, wout, b2 = arrays
    block_rows = entry_cell.shape[1] // n_sub
    cells, channels = vol.shape
    hidden = cot.shape[1]
    groups = n_sub // GROUP
    entries = GROUP * block_rows
    rows, named = (a.reshape(groups, 1, entries) for a in (entry_row, entry_cell))
    benc, b1, b2 = (a.reshape(1, hidden) for a in (benc, b1, b2))
    far = (named, win, b1, vol, wenc, wmid, wout, cot, rows, benc, b2)
    far = [pltpu.with_memory_space_constraint(a, pltpu.HBM) for a in far]
    return call(
        functools.partial(early_kernel, block_rows),
        [shape(a.shape, a.dtype) for a in far[3:]]
        + [
            shape((groups, cells, entries)),
            shape((cells, channels), F32),
            shape((cells, hidden), F32),
        ],
        [SMEM, SMEM] + [HBM] * 11,
        count,
        after,
        *far,
        scratch=[pltpu.VMEM(a.shape, a.dtype) for a in far[:3]] + [pltpu.SemaphoreType.DMA((11,))],
        flops=1 << 30,
    )


def compute(place, owner, pieces, early, n_sub):
    vol, wenc, wmid, wout, cot, rows = early[:6]
    cells, channels = vol.shape
    hidden = cot.shape[1]
    groups, _, entries = rows.shape
    block_rows = entries // GROUP
    message = (block_rows // 4 + 16, hidden)
    messages = [shape(message)] * n_sub if len(pieces) > 1 else [shape((n_sub,) + message)]
    keep, send, *messages = call(
        functools.partial(main_kernel, len(pieces), len(messages)),
        [shape((8, 80, hidden))] * 2 + messages,
        [SMEM] * 2 + [VMEM] * (len(pieces) + 11),
        place,
        owner,
        *pieces,
        *early,
        scratch=[pltpu.VMEM((cells, hidden), BF16)] * 4
        + [
            pltpu.VMEM((groups, entries, channels), BF16),
            pltpu.VMEM((groups, entries, hidden), BF16),
            pltpu.VMEM((n_sub, block_rows, channels), BF16),
            pltpu.VMEM((groups, entries, hidden), F32),
            pltpu.VMEM((cells, hidden), F32),
            pltpu.VMEM((n_sub, block_rows // 4, hidden), BF16),
            pltpu.VMEM((8, hidden), F32),
        ],
        flops=1 << 31,
        limit=32 * 1024 * 1024,
    )
    return keep, send, messages


def swap(value, axis, mask, size):
    return lax.ppermute(value, axis, [(i, i ^ mask) for i in range(size)])


def on_block(surface, owner, local, count, entry_row, entry_cell, arrays):
    region, me = lax.axis_index("region"), lax.axis_index("sub")
    core, chip = region % 2, region // 2
    n_sub = owner.shape[0]
    block_rows = entry_row.shape[1] // n_sub
    channels = surface.shape[1]
    hidden = arrays[1].shape[1]
    along_z = range(1, n_sub)

    request = jnp.concatenate([owner, local]).reshape(1, 2 * n_sub)
    requests = [request] + [swap(request, "sub", m, n_sub) for m in along_z]
    near = swap(surface, "region", 1, 4)
    *blocks, ids = call(
        serve_kernel,
        [shape((block_rows, channels))] * n_sub + [shape((n_sub,), jnp.int32)],
        [SMEM] * (n_sub + 1) + [VMEM],
        me.reshape(1),
        *requests,
        near,
        out_specs=[VMEM] * n_sub + [SMEM],
    )
    blocks = [blocks[0]] + [swap(blocks[m], "sub", m, n_sub) for m in along_z]
    early = prepare(count, ids, entry_row, entry_cell, n_sub, arrays)
    keep, send, messages = compute(jnp.stack([core, me]), owner, blocks, early, n_sub)
    got = swap(send, "region", 1, 4)
    keep, send = call(
        halve_kernel, [shape((4, 80, hidden))] * 2, [SMEM, VMEM, VMEM], chip.reshape(1), keep, got
    )
    got = swap(send, "region", 2, 4)
    messages = [messages[0]] + [swap(messages[m], "sub", m, n_sub) for m in along_z]
    terms = call(
        label_kernel,
        shape((n_sub,) + messages[0].shape),
        [SMEM] + [VMEM] * n_sub,
        ids,
        *messages,
    )
    shards = call(
        split_kernel,
        [shape((80, hidden))] * n_sub,
        [SMEM, VMEM, VMEM] + [ANY] * 3,
        me.reshape(1),
        keep,
        got,
        *messages[1:],
    )
    shards = [shards[0]] + [swap(shards[m], "sub", m, n_sub) for m in along_z]
    terms_x = swap(terms, "region", 2, 4)
    total = call(sum_kernel, shape((80, hidden)), [ANY] + [VMEM] * n_sub, terms_x, *shards)
    totals = [total] + [swap(total, "sub", m, n_sub) for m in along_z]
    terms = [terms, terms_x, swap(terms, "region", 1, 4), swap(terms_x, "region", 1, 4)]
    own = call(join_kernel, shape((n_sub, 80, hidden)), [SMEM] + [VMEM] * n_sub, me.reshape(1), *totals)
    over_x = swap(own, "region", 2, 4)
    surf, benc, b1, b2, passed = call(
        surface_kernel,
        [shape((surface.shape[0] // block_rows, block_rows, channels), F32)]
        + [shape((1, hidden), F32)] * 3
        + [shape(own.shape)],
        [VMEM] * 5,
        *terms,
        own,
    )
    over_core = swap(passed, "region", 1, 4)
    over_both = swap(over_x, "region", 1, 4)
    place = jnp.stack([core, chip])
    grads = [shape((8, 16, hidden))] * 2 + [shape((16, 32, hidden))] * 2
    some = call(
        weights_kernel,
        grads,
        [SMEM] + [VMEM] * 3,
        place,
        own,
        over_x,
        over_core,
        out_specs=[HBM] * 4,
        scratch=[pltpu.SemaphoreType.DMA((9,))],
        flops=1 << 30,
    )
    wenc, win, wmid, wout = call(
        last_weights_kernel,
        grads,
        [SMEM, VMEM] + [HBM] * 4,
        place,
        over_both,
        *some,
        out_specs=[HBM] * 4,
        scratch=[pltpu.SemaphoreType.DMA((3,))],
        aliases={2 + i: i for i in range(4)},
    )
    return (
        surf.reshape(surface.shape),
        wenc.reshape(128, hidden),
        benc.reshape(hidden),
        win.reshape(128, hidden),
        wmid.reshape(512, hidden),
        b1.reshape(hidden),
        wout.reshape(512, hidden),
        b2.reshape(hidden),
    )


def on_any(surface, owner, local, count, entry_row, entry_cell, arrays):
    n_sub = owner.shape[0]
    block_rows = entry_row.shape[1] // n_sub
    channels = surface.shape[1]
    hidden = arrays[1].shape[1]
    to_all = functools.partial(lax.all_to_all, axis_name="sub", split_axis=0, concat_axis=0, tiled=True)
    wanted = jnp.zeros((n_sub,), jnp.int32).at[owner].set(local)
    asked = to_all(wanted)
    stored = surface.reshape(surface.shape[0] // block_rows, block_rows, channels)
    fetched = to_all(jnp.take(stored, asked, axis=0))
    keep, send, (messages,) = compute(
        jnp.zeros((2,), jnp.int32),
        owner,
        [fetched],
        prepare(count, asked, entry_row, entry_cell, n_sub, arrays),
        n_sub,
    )
    bias = messages[0, block_rows // 4 :].astype(F32)
    bias = bias[0:8] + bias[8:16]
    surf = to_all(messages[:, : block_rows // 4]).astype(F32).reshape(n_sub, block_rows // 4, 4, channels)
    surf = surf.transpose(0, 2, 1, 3).reshape(n_sub, block_rows, channels)
    surf = jnp.zeros(stored.shape, F32).at[asked].add(surf).reshape(surface.shape)
    shards, bias = lax.psum(
        (jnp.concatenate([keep, send]).astype(F32), bias), ("region", "sub")
    )
    shards = shards.astype(BF16)
    small = shards[:, 64:80].reshape(256, hidden)
    return (
        lax.psum(surf, "region"),
        small[128:],
        bias[0],
        small[:128],
        shards[:, 32:64].reshape(512, hidden),
        bias[1],
        shards[:, 0:32].reshape(512, hidden),
        bias[2],
    )


def per_device(
    vol_feat,
    cotangent,
    surface,
    enc_weight,
    enc_bias,
    in_weight,
    mid_weight,
    first_bias,
    out_weight,
    second_bias,
    block_owner,
    block_local,
    block_count,
    entry_row,
    entry_cell,
):
    arrays = (
        vol_feat,
        cotangent,
        enc_weight,
        enc_bias,
        in_weight,
        mid_weight,
        first_bias,
        out_weight,
        second_bias,
    )
    small = lax.axis_size("region") == 4 and lax.axis_size("sub") == 4
    run = on_block if small else on_any
    return run(
        surface, block_owner[0], block_local[0], block_count, entry_row, entry_cell, arrays
    )


def solution(mesh):
    by_cell = P(("case", "region", "sub"), None)
    in_specs = (
        (by_cell, by_cell, P(("case", "sub"), None))
        + (P(),) * 7
        + (by_cell, by_cell, P(("case", "region", "sub")), by_cell, by_cell)
    )
    rows, line = P("case", None), P("case")
    out_specs = (P(("case", "sub"), None), rows, line, rows, rows, line, rows, line)
    return jax.shard_map(
        per_device, mesh=mesh, in_specs=in_specs, out_specs=out_specs, check_vma=False
    )
```
